512 devices in a mesh: grid: 128 (over y, z, core), slab: 4 (over x).
Axes of the slice: x: 4, y: 8, z: 8, core: 2. Of those that a mesh axis runs over, the one named last changes fastest.
Arguments:
- start_block: float32 [5, 64, 65536], P(None, None, ('grid', 'slab')), may hold values from -6 to 6
- jacobian: float32 [1024, 4, 5, 5, 64], P(('grid', 'slab')), may hold values from -1.5 to 1.5
- block_cols: int32 [1024, 4], P(('grid', 'slab')), may hold values from 0 to 3, as said below
- donor_cell: int32 [65536, 8], P(('grid', 'slab')), may hold values from 0 to 127
- donor_weight: float32 [65536, 8], P(('grid', 'slab')), may hold values from 0.05 to 0.25
- fringe_dest: int32 [65536, 1], P(('grid', 'slab')), may hold values from 0 to 127; in each aligned block of 128 rows (0 to 127, 128 to 255, ...) at most 2 rows name the same one
- recv_cell: int32 [65536], P(('grid', 'slab')), may hold values from 0 to 127
Outputs:
- basis: float32 [2, 5, 64, 65536], P(None, None, None, ('grid', 'slab'))
- projection: float32 [64, 128], replicated
- factor: float32 [128, 128], replicated
The draws below stay inside these ranges and needn't reach their ends.
Inputs may be any that keep to these rules, and one draw needn't show every extreme that they name: `block_cols`: the first entry of each block row is its own block (its index within the device plus 1); the first block row of every device lists block 0 and the last lists block 3 as second entry. `fringe_dest`: the 128 fringe cells of one device name any one grid index at most 2 times.
All inputs are finite; a program needn't handle non-finite values.
Results may differ from the reference program's by a relative error of at most 0.0003.
Values sent between devices are 32-bit elements; how exact they have to be, the bound alone decides.
A program may use at most 64 MiB of HBM per device.

```python
import math
import jax
import jax.numpy as jnp
import numpy as np
from jax import lax

VARS = 5
RHS = 64
BLK = 64
KNB = 4
STEN = 8
NBLK = 2
FR = 128
CAP = 2
CELLS = 128
NBLK_ALL = 1024
ALLCELLS = 65536
FR_ALL = 65536
ROWS_ALL = 327680
N_GRID = 128
N_SLAB = 4


def draw_block_cols(key, part):
    key = jax.random.fold_in(key, 7)
    columns = jax.random.randint(key, (NBLK_ALL, KNB), 0, NBLK + 2, dtype=jnp.int32)
    local = jnp.arange(NBLK_ALL, dtype=jnp.int32) % NBLK
    columns = columns.at[:, 0].set(local + 1)
    second = jnp.where(local == 0, 0, jnp.where(local == NBLK - 1, NBLK + 1, columns[:, 1]))
    columns = columns.at[:, 1].set(second.astype(jnp.int32))
    return columns


def touch_ends(entries, rng, least, largest):
    longest = entries.shape.index(max(entries.shape))
    spots = []
    for shift in (0, 1):
        where = [jax.random.randint(jax.random.fold_in(rng, axis), (), 0, length) for axis, length in enumerate(entries.shape)]
        where[longest] = (where[longest] + shift) % entries.shape[longest]
        spots.append(tuple(where))
    return entries.at[spots[0]].set(least).at[spots[1]].set(largest)


def block_levels(key, shape, split, least, largest):
    factor_of, own = 1.0, jax.random.fold_in(key, 6)
    for position, blocks in split:
        steps = jnp.exp(jax.random.uniform(jax.random.fold_in(own, position), (blocks,), jnp.float32, least / len(split), largest / len(split)))
        factor_of = factor_of * jnp.repeat(steps, shape[position] // blocks).reshape([-1 if axis == position else 1 for axis in range(len(shape))])
    return factor_of


def deal_out(stream_key, own, number, rows, amount, top, limit, skew):
    ranking = jax.random.permutation(stream_key, amount)
    heavy_load, common = load_shares(amount, rows * top, limit, skew, True), load_shares(amount, rows * top, limit, skew, False)
    places = jnp.arange(amount)

    def named(tallies, turn):
        used = int((tallies > 0).sum())
        fixed = max(1, used // 4)
        shifted = fixed + (places - fixed + turn * (used - fixed)) % max(1, amount - fixed)
        return jnp.zeros((amount,), jnp.int32).at[ranking[jnp.where(places < fixed, places, shifted)]].set(jnp.asarray(tallies, jnp.int32))

    tallies = jnp.where(number % 4 == 0, named(heavy_load, number // 4), named(common, number - number // 4 - 1))
    mixed = jax.random.permutation(jax.random.fold_in(own, 3), amount)
    donor, taker = mixed[0:amount // 2 * 2:2], mixed[1:amount // 2 * 2:2]
    room = jnp.minimum(tallies[donor] - 1, limit - tallies[taker]) // 2
    room = jnp.where((donor == ranking[0]) | (taker == ranking[0]) | (tallies[taker] == 0), 0, jnp.maximum(room, 0))
    shifted = jax.random.randint(jax.random.fold_in(own, 4), (amount // 2,), 0, 1 << 20) % (room + 1)
    tallies = tallies.at[donor].add(-shifted).at[taker].add(shifted)
    labels = jnp.searchsorted(jnp.cumsum(tallies), jnp.arange(rows * top), side="right").astype(jnp.int32)
    listing = labels.reshape(top, rows).T
    listing = listing[jax.random.permutation(jax.random.fold_in(own, 1), rows)]
    turn = jax.random.randint(jax.random.fold_in(own, 2), (rows, 1), 0, top)
    return jnp.take_along_axis(listing, (jnp.arange(top)[None, :] + turn) % top, axis=1)


def load_shares(count, total, most, lean, full):
    weights = [(1 << 20) // math.isqrt(rank ** lean) + 1 for rank in range(1, count + 1)]
    largest = most if full else min(most, max(-(-total // count), total * weights[0] // sum(weights)))
    least = 1 if total - largest >= count - 1 else 0
    given, surplus = [largest] + [least] * (count - 1), total - largest - least * (count - 1)
    while surplus > 0:
        free = [i for i in range(1, count) if given[i] < largest] or [i for i in range(1, count) if given[i] < most]
        mass, remaining = sum([weights[i] for i in free]), surplus
        for i in free:
            extra = min(most - given[i], max(1, remaining * weights[i] // mass), surplus)
            given[i] = given[i] + extra
            surplus = surplus - extra
    return np.array(given)


def centred(stream_key, shape, scale, limit, shards=(), held_as=jnp.bfloat16):
    array = scale * jax.random.normal(stream_key, shape, jnp.float32)
    if shards:
        array = array * block_levels(stream_key, shape, shards, -0.22, 0.18)
    return jnp.clip(array, -limit, limit).astype(held_as)


def setup_inputs(seed: int = 0) -> dict:
    key_of = jax.random.split(jax.random.key(seed), 8)
    start_block = centred(key_of[0], (VARS, RHS, ALLCELLS), 1.0, 6.0, ((2, 512),), jnp.float32)
    jacobian = centred(key_of[1], (NBLK_ALL, KNB, VARS, VARS, BLK), 0.1, 1.5, ((0, 512),), jnp.float32)
    block_cols = draw_block_cols(jax.random.fold_in(key_of[7], 71), 0)
    donor_cell = touch_ends(jax.random.randint(key_of[3], (FR_ALL, STEN), 0, CELLS), jax.random.fold_in(key_of[3], 1), 0, CELLS - 1).astype(jnp.int32)
    donor_weight = jnp.clip(0.05 + 0.2 * jax.random.uniform(key_of[4], (FR_ALL, STEN), jnp.float32) ** block_levels(key_of[4], (FR_ALL, STEN), ((0, 512),), -0.2, 0.2), 0.05, 0.25)
    fringe_dest_keys = jax.random.split(jax.random.fold_in(key_of[5], 1), FR_ALL // FR)
    fringe_dest_turns = jax.random.permutation(jax.random.fold_in(key_of[5], 3), FR_ALL // FR)
    fringe_dest = jax.vmap(lambda own, number: deal_out(jax.random.fold_in(key_of[5], 2), own, number, FR, N_GRID, 1, CAP, 2))(fringe_dest_keys, fringe_dest_turns).reshape((FR_ALL, 1))
    recv_cell = touch_ends(jax.random.randint(key_of[6], (FR_ALL,), 0, CELLS), jax.random.fold_in(key_of[6], 1), 0, CELLS - 1).astype(jnp.int32)
    return {"start_block": start_block, "jacobian": jacobian, "block_cols": block_cols, "donor_cell": donor_cell, "donor_weight": donor_weight, "fringe_dest": fringe_dest, "recv_cell": recv_cell}


def apply_operator(field, jacobian, block_cols, donor_cell, donor_weight, fringe_dest, recv_cell):
    dev_count = N_GRID * N_SLAB
    blocks = field.reshape(VARS, RHS, dev_count, NBLK, BLK)
    slab_pos = jnp.arange(dev_count, dtype=jnp.int32) % N_SLAB
    has_prev = (slab_pos > 0).astype(field.dtype)[:, None]
    has_next = (slab_pos < N_SLAB - 1).astype(field.dtype)[:, None]
    before = jnp.roll(blocks[:, :, :, NBLK - 1, :], 1, axis=2) * has_prev
    after = jnp.roll(blocks[:, :, :, 0, :], -1, axis=2) * has_next
    padded = jnp.concatenate([before[:, :, :, None], blocks, after[:, :, :, None]], axis=3)
    jac_dev = jacobian.reshape(dev_count, NBLK, KNB, VARS, VARS, BLK)
    cols_dev = block_cols.reshape(dev_count, NBLK, KNB)
    result = blocks
    for column in range(KNB):
        picked = jax.vmap(lambda part, index: jnp.take(part, index, axis=2), in_axes=(2, 0), out_axes=2)(padded, cols_dev[:, :, column])
        result = result + jnp.einsum('diabc,brdic->ardic', jac_dev[:, :, column], picked, precision=lax.Precision.HIGHEST)
    result = result.reshape(VARS * RHS, ALLCELLS)
    flat = field.reshape(VARS * RHS, ALLCELLS)
    owner = jnp.arange(FR_ALL, dtype=jnp.int32) // FR
    source = owner[:, None] * CELLS + donor_cell
    values = jnp.sum(flat[:, source] * donor_weight[None], axis=2)
    target = ((fringe_dest[:, 0] * N_SLAB + owner % N_SLAB) * CELLS + recv_cell).astype(jnp.int32)
    result = result.at[:, target].add(values)
    return result.reshape(VARS, RHS, ALLCELLS)

def reference(start_block, jacobian, block_cols, donor_cell, donor_weight, fringe_dest, recv_cell):
    first = apply_operator(start_block, jacobian, block_cols, donor_cell, donor_weight, fringe_dest, recv_cell)
    second = apply_operator(first, jacobian, block_cols, donor_cell, donor_weight, fringe_dest, recv_cell)
    stacked = jnp.stack([first, second])
    projection = jnp.einsum('vrc,jvsc->rjs', start_block, stacked, precision=lax.Precision.HIGHEST) / ROWS_ALL
    projected = stacked - jnp.einsum('vrc,rjs->jvsc', start_block, projection, precision=lax.Precision.HIGHEST)
    gram = jnp.einsum('jvrc,kvsc->jrks', projected, projected, precision=lax.Precision.HIGHEST).reshape(2 * RHS, 2 * RHS) / ROWS_ALL
    lower = jnp.linalg.cholesky(gram)
    columns = jnp.transpose(projected, (0, 2, 1, 3)).reshape(2 * RHS, VARS * ALLCELLS)
    solved = lax.linalg.triangular_solve(lower, columns, left_side=True, lower=True)
    basis = jnp.transpose(solved.reshape(2, RHS, VARS, ALLCELLS), (0, 2, 1, 3))
    return (basis, projection.reshape(RHS, 2 * RHS), lower.T)
```

```python
import functools

import jax
import jax.numpy as jnp
from jax import lax
from jax.experimental import pallas as pl
from jax.experimental.pallas import tpu as pltpu
from jax.sharding import PartitionSpec as P

MESH = pl.DeviceIdType.MESH
F32 = jnp.float32
BF16 = jnp.bfloat16
NT = (((1,), (1,)), ((), ()))
NN = (((1,), (0,)), ((), ()))
TN = (((0,), (0,)), ((), ()))
LANES = 128
HALF = 64
PACK = 32


def halves(x):
    high = x.astype(BF16)
    return high, (x - high.astype(F32)).astype(BF16)


def dot1(a, b, dims):
    return lax.dot_general(a, b, dims, preferred_element_type=F32)


def dot3(a, b, dims):
    ah, al = halves(a)
    bh, bl = halves(b)
    return dot1(ah, bh, dims) + (dot1(ah, bl, dims) + dot1(al, bh, dims))


def lane_ids(shape):
    return lax.broadcasted_iota(jnp.int32, shape, len(shape) - 1)


def row_ids(shape):
    return lax.broadcasted_iota(jnp.int32, shape, len(shape) - 2)


def swap_halves(x):
    return pltpu.roll(x, HALF, x.ndim - 1)


def wide(field):
    return jnp.concatenate([field[v] for v in range(field.shape[0])], axis=1)


def split_rows(packed):
    return jnp.concatenate([packed[:, :HALF], packed[:, HALF:]], axis=0)


def eliminate(gram):
    size = gram.shape[0]
    eye = (row_ids((size, size)) == lane_ids((size, size))).astype(F32)
    work = jnp.concatenate([gram, eye], axis=1)
    blocks = [work[8 * i:8 * i + 8] for i in range(size // 8)]
    sub = row_ids((8, LANES))
    done = []
    for kb in range(len(blocks)):
        cols = {
            i: [jnp.broadcast_to(blocks[i][:, 8 * kb + t:8 * kb + t + 1], (8, LANES)) for t in range(8)]
            for i in range(kb, len(blocks))
        }
        pivots = jnp.ones((8, LANES), F32)
        for t in range(8):
            row = jnp.broadcast_to(blocks[kb][t:t + 1], (8, LANES))
            heads = [jnp.broadcast_to(cols[kb][u][t:t + 1], (8, LANES)) for u in range(t, 8)]
            inverse = 1.0 / heads[0]
            pivots = jnp.where(sub == t, heads[0], pivots)
            for i in range(kb, len(blocks)):
                ratio = cols[i][t] * inverse
                if i == kb:
                    ratio = jnp.where(sub > t, ratio, 0.0)
                for u in range(t + 1, 8):
                    cols[i][u] = cols[i][u] - ratio * heads[u - t]
                blocks[i] = blocks[i] - ratio * row
        done.append(blocks[kb] * lax.rsqrt(pivots))
    both = jnp.concatenate(done, axis=0)
    upper = jnp.where(row_ids((size, size)) <= lane_ids((size, size)), both[:, :size], 0.0)
    return upper, both[:, size:]


class Sizes:
    def __init__(self, grid, slab, low, total_rows):
        self.grid, self.slab, self.low = grid, slab, low
        self.high = grid // low
        self.first = self.high * slab
        self.share = PACK // self.first
        self.total_rows = total_rows


def kernel(
    sz, cols_ref, x_ref, jac_ref, cell_ref, weight_ref, dest_ref, recv_ref,
    basis_ref, proj_ref, factor_ref,
    w1_ref, w2_ref, jeff_ref, send1, send2, got1, got2, place_ref, scatter_ref,
    edge_out1, edge_in1, edge_out2, edge_in2,
    part_e, a_e, mid_e, b_e, sum_e, all_e,
    part_l, a_l, mid_l, b_l, sum_l, all_l,
    fr_send, fr_recv, ed_send, ed_recv, red_send, red_recv,
):
    var_count = x_ref.shape[0]
    g = lax.axis_index("grid")
    s = lax.axis_index("slab")
    hi = lax.div(g, sz.low)
    lo = lax.rem(g, sz.low)
    me1 = hi * sz.slab + s

    def first_peer(i):
        q = lax.rem(me1 + i, sz.first)
        return q, (lax.div(q, sz.slab) * sz.low + lo, lax.rem(q, sz.slab))

    def second_peer(i):
        q = lax.rem(lo + i, sz.low)
        return q, (hi * sz.low + q, s)

    if sz.grid < LANES:
        got1[...] = jnp.zeros_like(got1)
        got2[...] = jnp.zeros_like(got2)

    barrier = pltpu.get_barrier_semaphore()

    def greet_grid(i, carry):
        pl.semaphore_signal(barrier, inc=1, device_id=(lax.rem(g + i, sz.grid), s), device_id_type=MESH)
        return carry

    lax.fori_loop(1, sz.grid, greet_grid, 0)

    def greet_slab(i, carry):
        peer_s = lax.rem(s + 1 + lax.div(i, sz.high), sz.slab)
        peer_h = lax.rem(i, sz.high)
        pl.semaphore_signal(barrier, inc=1, device_id=(peer_h * sz.low + lo, peer_s), device_id_type=MESH)
        return carry

    lax.fori_loop(0, (sz.slab - 1) * sz.high, greet_slab, 0)

    rows = cell_ref.shape[0]
    lanes = lane_ids((rows, LANES))
    weight_mat = jnp.zeros((rows, LANES), F32)
    for t in range(cell_ref.shape[1]):
        weight_mat += jnp.where(cell_ref[:, t:t + 1] == lanes, weight_ref[:, t:t + 1], 0.0)
    named = dest_ref[...] == lanes
    earlier = (lane_ids((rows, rows)) < row_ids((rows, rows))).astype(BF16)
    rank = dot1(earlier, named.astype(BF16), NN)
    slots = jnp.concatenate(
        [jnp.where(named, (rank == float(j)).astype(F32), 0.0) for j in range(2)], axis=1
    ).astype(BF16)
    on_diagonal = row_ids((rows, rows)) == lane_ids((rows, rows))
    recv_col = jnp.sum(jnp.where(on_diagonal, recv_ref[...].astype(F32) + 1.0, 0.0), axis=1, keepdims=True)
    table = jnp.concatenate([weight_mat, jnp.broadcast_to(recv_col, (rows, LANES))], axis=1)
    th, tl = halves(table)
    placed = dot1(slots, th, TN) + dot1(slots, tl, TN)
    place_ref[...] = jnp.concatenate([placed[:LANES, :LANES], placed[LANES:, :LANES]], axis=1)
    cell_row = jnp.where(lanes < HALF, placed[:LANES, LANES:], placed[LANES:, LANES:])

    def fill_fringe(field_ref, out_ref):
        zero = jnp.zeros((HALF, LANES), F32)
        blocks = []
        for v in range(var_count):
            x = field_ref[v]
            blocks += [jnp.concatenate([x, zero], axis=1), jnp.concatenate([zero, x], axis=1)]
        out = dot3(place_ref[...], jnp.concatenate(blocks, axis=0), NT)
        for v in range(var_count):
            out_ref[:, v, :] = out[:, LANES * v:LANES * (v + 1)]

    def fill_edges(field_ref, out_ref):
        low_half = lane_ids((PACK, LANES)) < HALF
        for v in range(var_count):
            top, bottom = field_ref[v, :PACK, :], field_ref[v, PACK:, :]
            out_ref[0, v] = jnp.where(low_half, swap_halves(top), bottom)
            out_ref[1, v] = jnp.where(low_half, top, swap_halves(bottom))

    def start_edges(out_ref, in_ref, which):
        for side, step in ((0, 1), (1, sz.slab - 1)):
            pltpu.make_async_remote_copy(
                src_ref=out_ref.at[side], dst_ref=in_ref.at[side],
                send_sem=ed_send.at[2 * which + side], recv_sem=ed_recv.at[2 * which + side],
                device_id=(g, lax.rem(s + step, sz.slab)), device_id_type=MESH,
            ).start()

    def wait_edges(ref, sems, which):
        for side in range(2):
            pltpu.make_async_copy(ref.at[side], ref.at[side], sems.at[2 * which + side]).wait()

    def start_fringe(out_ref, in_ref, which):
        def body(i, carry):
            p = lax.rem(g + i * 37, sz.grid)
            pltpu.make_async_remote_copy(
                src_ref=out_ref.at[p], dst_ref=in_ref.at[g],
                send_sem=fr_send.at[which], recv_sem=fr_recv.at[which],
                device_id=(p, s), device_id_type=MESH,
            ).start()
            return carry

        lax.fori_loop(1, sz.grid, body, 0)

    def wait_many(ref, count, sem):
        pltpu.make_async_copy(ref.at[pl.ds(0, count)], ref.at[pl.ds(0, count)], sem).wait()

    def own_terms(field_ref, out_ref):
        low_half = lane_ids((HALF, LANES)) < HALF
        for v in range(var_count):
            x = field_ref[v]
            flipped = swap_halves(x)
            left, right = jnp.where(low_half, x, flipped), jnp.where(low_half, flipped, x)
            for a in range(var_count):
                term = jeff_ref[1, a, v:v + 1, :] * left + jeff_ref[2, a, v:v + 1, :] * right
                base = field_ref[a] if v == 0 else out_ref[a]
                out_ref[a] = base + term

    def edge_terms(in_ref, out_ref):
        low_half = lane_ids((PACK, LANES)) < HALF
        for v in range(var_count):
            spread = []
            for side in range(2):
                packed = in_ref[side, v]
                flipped = swap_halves(packed)
                spread.append(jnp.concatenate(
                    [jnp.where(low_half, packed, flipped), jnp.where(low_half, flipped, packed)], axis=0))
            for a in range(var_count):
                term = jeff_ref[0, a, v:v + 1, :] * spread[0] + jeff_ref[3, a, v:v + 1, :] * spread[1]
                out_ref[a] = out_ref[a] + term

    def fringe_terms(in_ref, out_ref):
        left = []
        for v in range(var_count):
            turned = jnp.transpose(in_ref[:, v, :])
            left.append(jnp.concatenate([turned[:HALF], turned[HALF:]], axis=1))
        lh, ll = halves(jnp.concatenate(left, axis=0))
        scatter = scatter_ref[...]
        total = dot1(lh, scatter, NN) + dot1(ll, scatter, NN)
        for v in range(var_count):
            out_ref[v] = out_ref[v] + total[HALF * v:HALF * (v + 1)]

    fill_edges(x_ref, edge_out1)
    fill_fringe(x_ref, send1)
    send1[:, var_count, :] = cell_row
    got1[g] = send1[g]
    pl.semaphore_wait(barrier, sz.grid - 1 + (sz.slab - 1) * sz.high)
    start_edges(edge_out1, edge_in1, 0)
    start_fringe(send1, got1, 0)

    side_on = [(s > 0).astype(F32), F32(1.0), F32(1.0), (s < sz.slab - 1).astype(F32)]
    low_lane = lane_ids((1, LANES)) < HALF
    for a in range(var_count):
        sums = [jnp.zeros((var_count, LANES), F32) for _ in range(4)]
        for k in range(jac_ref.shape[1]):
            both = jnp.concatenate([jac_ref[0, k, a], jac_ref[1, k, a]], axis=1)
            for j in range(4):
                picks = [jnp.where(cols_ref[i, k] == j, side_on[j], F32(0.0)) for i in range(2)]
                sums[j] += jnp.where(low_lane, picks[0], picks[1]) * both
        for j in range(4):
            jeff_ref[j, a, 0:var_count, :] = sums[j]

    own_terms(x_ref, w1_ref)
    wait_edges(edge_in1, ed_recv, 0)
    edge_terms(edge_in1, w1_ref)
    wait_many(got1, sz.grid - 1, fr_recv.at[0])
    cells = got1[:, var_count, :]
    ids = (lanes + 1).astype(F32)
    scatter_ref[...] = jnp.concatenate(
        [(cells[:, j * HALF:j * HALF + 1] == ids).astype(F32) for j in range(2)], axis=0
    ).astype(BF16)
    fringe_terms(got1, w1_ref)

    fill_edges(w1_ref, edge_out2)
    start_edges(edge_out2, edge_in2, 1)
    fill_fringe(w1_ref, send2)
    got2[g] = send2[g]
    start_fringe(send2, got2, 1)

    def reduce_start(part, a_buf, which):
        mine = me1 * sz.share
        a_buf[me1] = part[pl.ds(mine, sz.share)]

        def body(i, carry):
            q, peer = first_peer(i)
            pltpu.make_async_remote_copy(
                src_ref=part.at[pl.ds(q * sz.share, sz.share)], dst_ref=a_buf.at[me1],
                send_sem=red_send.at[which], recv_sem=red_recv.at[which],
                device_id=peer, device_id_type=MESH,
            ).start()
            return carry

        lax.fori_loop(1, sz.first, body, 0)

    def reduce_middle(a_buf, mid, b_buf, which):
        wait_many(a_buf, sz.first - 1, red_recv.at[which])
        value = a_buf[0]
        for i in range(1, sz.first):
            value = value + a_buf[i]
        mid[...] = value
        b_buf[lo] = value

        def body(i, carry):
            _, peer = second_peer(i)
            pltpu.make_async_remote_copy(
                src_ref=mid, dst_ref=b_buf.at[lo],
                send_sem=red_send.at[which + 1], recv_sem=red_recv.at[which + 1],
                device_id=peer, device_id_type=MESH,
            ).start()
            return carry

        lax.fori_loop(1, sz.low, body, 0)

    def reduce_last(b_buf, sum_buf, all_buf, which):
        wait_many(b_buf, sz.low - 1, red_recv.at[which + 1])
        value = b_buf[0]
        for i in range(1, sz.low):
            value = value + b_buf[i]
        sum_buf[...] = value
        all_buf[me1] = value

        def body(i, carry):
            _, peer = first_peer(i)
            pltpu.make_async_remote_copy(
                src_ref=sum_buf, dst_ref=all_buf.at[me1],
                send_sem=red_send.at[which + 2], recv_sem=red_recv.at[which + 2],
                device_id=peer, device_id_type=MESH,
            ).start()
            return carry

        lax.fori_loop(1, sz.first, body, 0)

    def reduced(all_buf, which):
        wait_many(all_buf, sz.first - 1, red_recv.at[which + 2])
        scale = 1.0 / sz.total_rows
        return [all_buf[:, :, t, :].reshape(PACK, LANES) * scale for t in range(3)]

    low_half = lane_ids((PACK, LANES)) < HALF
    wide_x = wide(x_ref)
    wide_1 = wide(w1_ref)
    pair = jnp.concatenate([wide_x, wide_1], axis=0)
    early = dot3(pair, pair, NT)
    part_e[:, 0, :] = early[:PACK]
    part_e[:, 1, :] = early[PACK:HALF]
    part_e[:, 2, :] = jnp.where(low_half, swap_halves(early[HALF:HALF + PACK]), early[HALF + PACK:])
    reduce_start(part_e, a_e, 0)
    own_terms(w1_ref, w2_ref)
    reduce_middle(a_e, mid_e, b_e, 0)
    wait_edges(edge_in2, ed_recv, 1)
    edge_terms(edge_in2, w2_ref)
    reduce_last(b_e, sum_e, all_e, 0)
    wait_many(got2, sz.grid - 1, fr_recv.at[1])
    fringe_terms(got2, w2_ref)

    wide_2 = wide(w2_ref)
    late = dot3(jnp.concatenate([wide_x, wide_1, wide_2], axis=0), wide_2, NT)
    for t in range(3):
        block = late[HALF * t:HALF * (t + 1)]
        part_l[:, t, :] = jnp.concatenate([block[:PACK], block[PACK:]], axis=1)
    reduce_start(part_l, a_l, 3)

    top, bottom, third = reduced(all_e, 0)
    own = jnp.concatenate([top[:, :HALF], bottom[:, :HALF]], axis=0)
    proj_1 = jnp.concatenate([top[:, HALF:], bottom[:, HALF:]], axis=0)
    reduce_middle(a_l, mid_l, b_l, 3)
    twice_1 = 2.0 * proj_1 - dot3(own, proj_1, NN)
    gram_11 = split_rows(third) - dot3(proj_1, twice_1, TN)
    factor_11, inverse_11 = eliminate(gram_11)
    reduce_last(b_l, sum_l, all_l, 3)
    projected_1 = wide_1 - dot3(proj_1, wide_x, TN)
    basis_1 = dot3(inverse_11, projected_1, NN)
    for v in range(var_count):
        basis_ref[0, v] = basis_1[:, LANES * v:LANES * (v + 1)]

    proj_2, cross, square = [split_rows(x) for x in reduced(all_l, 3)]
    twice_2 = 2.0 * proj_2 - dot3(own, proj_2, NN)
    gram_12 = cross - dot3(twice_1, proj_2, TN)
    gram_22 = square - dot3(proj_2, twice_2, TN)
    factor_12 = dot3(inverse_11, gram_12, NN)
    factor_22, inverse_22 = eliminate(gram_22 - dot3(factor_12, factor_12, TN))
    projected_2 = wide_2 - dot3(proj_2, wide_x, TN) - dot3(factor_12, basis_1, TN)
    basis_2 = dot3(inverse_22, projected_2, NN)
    for v in range(var_count):
        basis_ref[1, v] = basis_2[:, LANES * v:LANES * (v + 1)]
    proj_ref[...] = jnp.concatenate([proj_1, proj_2], axis=1)
    factor_ref[...] = jnp.concatenate([
        jnp.concatenate([factor_11, factor_12], axis=1),
        jnp.concatenate([jnp.zeros((HALF, HALF), F32), factor_22], axis=1),
    ], axis=0)

    wait_edges(edge_out1, ed_send, 0)
    wait_edges(edge_out2, ed_send, 1)
    wait_many(send1, sz.grid - 1, fr_send.at[0])
    wait_many(send2, sz.grid - 1, fr_send.at[1])
    for which, (a_buf, b_buf, all_buf) in ((0, (a_e, b_e, all_e)), (3, (a_l, b_l, all_l))):
        wait_many(a_buf, sz.first - 1, red_send.at[which])
        wait_many(b_buf, sz.low - 1, red_send.at[which + 1])
        wait_many(all_buf, sz.first - 1, red_send.at[which + 2])


def shards(sz, start_block, jacobian, block_cols, donor_cell, donor_weight, fringe_dest, recv_cell):
    var_count, rhs_count, cell_count = start_block.shape
    vmem = pl.BlockSpec(memory_space=pltpu.VMEM)
    smem = pl.BlockSpec(memory_space=pltpu.SMEM)
    field = (var_count, rhs_count, cell_count)
    edge = pltpu.VMEM((2, var_count, PACK, LANES), F32)
    sums = [
        pltpu.VMEM((PACK, 3, LANES), F32),
        pltpu.VMEM((sz.first, sz.share, 3, LANES), F32),
        pltpu.VMEM((sz.share, 3, LANES), F32),
        pltpu.VMEM((sz.low, sz.share, 3, LANES), F32),
        pltpu.VMEM((sz.share, 3, LANES), F32),
        pltpu.VMEM((sz.first, sz.share, 3, LANES), F32),
    ]
    return pl.pallas_call(
        functools.partial(kernel, sz),
        out_shape=(
            jax.ShapeDtypeStruct((2,) + field, F32),
            jax.ShapeDtypeStruct((rhs_count, 2 * rhs_count), F32),
            jax.ShapeDtypeStruct((2 * rhs_count, 2 * rhs_count), F32),
        ),
        in_specs=[smem] + [vmem] * 6,
        out_specs=(vmem, vmem, vmem),
        scratch_shapes=[
            pltpu.VMEM(field, F32),
            pltpu.VMEM(field, F32),
            pltpu.VMEM((4, var_count, 8, LANES), F32),
            pltpu.VMEM((LANES, var_count + 1, LANES), F32),
            pltpu.VMEM((LANES, var_count, LANES), F32),
            pltpu.VMEM((LANES, var_count + 1, LANES), F32),
            pltpu.VMEM((LANES, var_count, LANES), F32),
            pltpu.VMEM((LANES, 2 * LANES), F32),
            pltpu.VMEM((2 * LANES, LANES), BF16),
            edge, edge, edge, edge,
            *sums, *sums,
            pltpu.SemaphoreType.DMA((2,)),
            pltpu.SemaphoreType.DMA((2,)),
            pltpu.SemaphoreType.DMA((4,)),
            pltpu.SemaphoreType.DMA((4,)),
            pltpu.SemaphoreType.DMA((6,)),
            pltpu.SemaphoreType.DMA((6,)),
        ],
        compiler_params=pltpu.CompilerParams(
            collective_id=0, has_side_effects=True, vmem_limit_bytes=32 * 1024 * 1024
        ),
    )(block_cols, start_block, jacobian, donor_cell, donor_weight, fringe_dest,
      recv_cell.reshape(1, recv_cell.shape[0]))


def solution(mesh):
    grid, slab = mesh.shape["grid"], mesh.shape["slab"]
    low = min(16, max(2, grid // 2))
    sz = Sizes(grid, slab, low, 5 * 128 * grid * slab)
    both = ("grid", "slab")
    in_specs = (
        P(None, None, both),
        P(both, None, None, None, None),
        P(both, None),
        P(both, None),
        P(both, None),
        P(both, None),
        P(both),
    )
    out_specs = (P(None, None, None, both), P(), P())
    return jax.shard_map(
        functools.partial(shards, sz), mesh=mesh, in_specs=in_specs, out_specs=out_specs, check_vma=False
    )
```

```python
import functools

import jax
import jax.numpy as jnp
from jax import lax
from jax.experimental import pallas as pl
from jax.experimental.pallas import tpu as pltpu
from jax.sharding import PartitionSpec as P

MESH = pl.DeviceIdType.MESH
F32 = jnp.float32
BF16 = jnp.bfloat16
NT = (((1,), (1,)), ((), ()))
NN = (((1,), (0,)), ((), ()))
TN = (((0,), (0,)), ((), ()))
LANES = 128
HALF = 64
PACK = 32
HBM = pltpu.HBM


def halves(x):
    high = x.astype(BF16)
    return high, (x - high.astype(F32)).astype(BF16)


def dot1(a, b, dims):
    return lax.dot_general(a, b, dims, preferred_element_type=F32)


def dot3(a, b, dims):
    ah, al = halves(a)
    bh, bl = halves(b)
    return dot1(ah, bh, dims) + (dot1(ah, bl, dims) + dot1(al, bh, dims))


def lane_ids(shape):
    return lax.broadcasted_iota(jnp.int32, shape, len(shape) - 1)


def row_ids(shape):
    return lax.broadcasted_iota(jnp.int32, shape, len(shape) - 2)


def swap_halves(x):
    return pltpu.roll(x, HALF, x.ndim - 1)


def wide(field):
    return jnp.concatenate([field[v] for v in range(field.shape[0])], axis=1)


def split_rows(packed):
    return jnp.concatenate([packed[:, :HALF], packed[:, HALF:]], axis=0)


def eliminate(gram):
    size = gram.shape[0]
    eye = (row_ids((size, size)) == lane_ids((size, size))).astype(F32)
    work = jnp.concatenate([gram, eye], axis=1)
    blocks = [work[8 * i:8 * i + 8] for i in range(size // 8)]
    sub = row_ids((8, LANES))
    done = []
    for kb in range(len(blocks)):
        cols = {
            i: [jnp.broadcast_to(blocks[i][:, 8 * kb + t:8 * kb + t + 1], (8, LANES)) for t in range(8)]
            for i in range(kb, len(blocks))
        }
        pivots = jnp.ones((8, LANES), F32)
        for t in range(8):
            row = jnp.broadcast_to(blocks[kb][t:t + 1], (8, LANES))
            heads = [jnp.broadcast_to(cols[kb][u][t:t + 1], (8, LANES)) for u in range(t, 8)]
            inverse = 1.0 / heads[0]
            pivots = jnp.where(sub == t, heads[0], pivots)
            for i in range(kb, len(blocks)):
                ratio = cols[i][t] * inverse
                if i == kb:
                    ratio = jnp.where(sub > t, ratio, 0.0)
                for u in range(t + 1, 8):
                    cols[i][u] = cols[i][u] - ratio * heads[u - t]
                blocks[i] = blocks[i] - ratio * row
        done.append(blocks[kb] * lax.rsqrt(pivots))
    both = jnp.concatenate(done, axis=0)
    upper = jnp.where(row_ids((size, size)) <= lane_ids((size, size)), both[:, :size], 0.0)
    return upper, both[:, size:]


class Sizes:
    def __init__(self, ny, nz, nc, ns, total_rows):
        self.ny, self.nz, self.nc, self.ns = ny, nz, nc, ns
        self.grid = ny * nz * nc
        self.first, self.second = nz * ns, ny * nc
        self.share = PACK // self.first
        self.total_rows = total_rows


CHUNKS = ((0,), (1, 2), (3, 4))


def ring(size):
    return sorted(range(size), key=lambda step: -min(step, size - step))


def kernel(sz, *refs):
    (cols_hbm, x_hbm, jac_hbm, cell_hbm, weight_hbm, dest_hbm, recv_hbm,
     basis_ref, proj_ref, factor_ref,
     cols_ref, x_ref, jac_ref, cell_ref, weight_ref, dest_ref, recv_ref, load_sem,
     w1_ref, w2_ref, jeff_ref, place_high, place_low, scatter_ref,
     edge_out1, edge_in1, edge_out2, edge_in2,
     part_e, a_e, mid_e, b_e, sum_e, all_e,
     part_l, a_l, mid_l, b_l, sum_l, all_l,
     fr_send, fr_recv, ed_send, ed_recv, red_send, red_recv, *fringe) = refs
    count = len(CHUNKS)
    send1, got1, send2, got2 = [fringe[k * count:(k + 1) * count] for k in range(4)]
    var_count = x_ref.shape[0]
    g = lax.axis_index("grid")
    s = lax.axis_index("slab")
    core = lax.rem(g, sz.nc)
    z = lax.rem(lax.div(g, sz.nc), sz.nz)
    y = lax.div(g, sz.nc * sz.nz)
    me1 = z * sz.ns + s
    me2 = y * sz.nc + core

    loads = {}
    for k, (name, source, target) in enumerate((
        ("dest", dest_hbm, dest_ref), ("cell", cell_hbm, cell_ref), ("weight", weight_hbm, weight_ref),
        ("recv", recv_hbm, recv_ref), ("x", x_hbm, x_ref), ("jac", jac_hbm, jac_ref), ("cols", cols_hbm, cols_ref),
    )):
        loads[name] = pltpu.make_async_copy(source, target, load_sem.at[k])
        loads[name].start()

    rows_of = [lax.rem(y + step, sz.ny) * (sz.nz * sz.nc) for step in ring(sz.ny)]
    columns_of = [lax.rem(z + step, sz.nz) * sz.nc for step in ring(sz.nz)]
    cores_of = [lax.rem(core + step, sz.nc) for step in ring(sz.nc)]
    slabs_of = [lax.rem(s + step, sz.ns) for step in ring(sz.ns)]
    plane_of = [column + part for column in columns_of for part in cores_of]
    first_of = [(column, slab) for column in columns_of for slab in slabs_of][:-1]
    second_of = [row + part for row in rows_of for part in cores_of][:-1]

    def each_grid_peer(act):
        def body(i, carry):
            row = lax.rem(y + sz.ny // 2 + lax.div(i + 1, 2) * (1 - 2 * lax.rem(i, 2)), sz.ny) * (sz.nz * sz.nc)
            for place in plane_of:
                act(row + place)
            return carry

        lax.fori_loop(0, sz.ny - 1, body, 0)
        for place in plane_of[:-1]:
            act(rows_of[-1] + place)

    if sz.grid < LANES:
        for ref in (*got1, *got2):
            ref[...] = jnp.zeros_like(ref)

    barrier = pltpu.get_barrier_semaphore()

    def greet(p):
        pl.semaphore_signal(barrier, inc=1, device_id=(p, s), device_id_type=MESH)

    each_grid_peer(greet)
    for step in range(1, sz.ns):
        pl.semaphore_signal(barrier, inc=1, device_id=(g, lax.rem(s + step, sz.ns)), device_id_type=MESH)

    rows = dest_ref.shape[1]
    ids = row_ids((LANES, rows))
    for name in ("dest", "cell", "weight", "recv"):
        loads[name].wait()
    named = dest_ref[...] == ids
    later = (row_ids((rows, rows)) < lane_ids((rows, rows))).astype(BF16)
    rank = dot1(named.astype(BF16), later, NN)
    slots = jnp.concatenate(
        [jnp.where(named, (rank == float(j)).astype(F32), 0.0) for j in range(2)], axis=0
    ).astype(BF16)
    weight_mat = jnp.zeros((LANES, rows), F32)
    for t in range(cell_ref.shape[0]):
        weight_mat += jnp.where(cell_ref[t:t + 1, :] == ids, weight_ref[t:t + 1, :], 0.0)
    numbers = jnp.broadcast_to(recv_ref[...].astype(F32) + 1.0, (LANES, rows))
    th, tl = halves(jnp.concatenate([weight_mat, numbers], axis=0))
    placed = dot1(slots, th, NT) + dot1(slots, tl, NT)
    place_high[...], place_low[...] = halves(
        jnp.concatenate([placed[:LANES, :LANES], placed[LANES:, :LANES]], axis=1))
    lanes = lane_ids((LANES, LANES))
    cell_row = jnp.where(lanes < HALF, placed[:LANES, LANES:], placed[LANES:, LANES:])

    def fill_fringe(field_ref, out_ref, chunk):
        zero = jnp.zeros((HALF, LANES), F32)
        blocks = []
        for v in chunk:
            field = field_ref[v]
            blocks += [jnp.concatenate([field, zero], axis=1), jnp.concatenate([zero, field], axis=1)]
        fh, fl = halves(jnp.concatenate(blocks, axis=0))
        ph, plow = place_high[...], place_low[...]
        out = dot1(ph, fh, NT) + (dot1(ph, fl, NT) + dot1(plow, fh, NT))
        for k in range(len(chunk)):
            out_ref[:, k, :] = out[:, LANES * k:LANES * (k + 1)]

    def fill_edges(field_ref, out_ref):
        low_half = lane_ids((PACK, LANES)) < HALF
        for v in range(var_count):
            top, bottom = field_ref[v, :PACK, :], field_ref[v, PACK:, :]
            out_ref[0, v] = jnp.where(low_half, swap_halves(top), bottom)
            out_ref[1, v] = jnp.where(low_half, top, swap_halves(bottom))

    def start_edges(out_ref, in_ref, which):
        for side, step in ((0, 1), (1, sz.ns - 1)):
            pltpu.make_async_remote_copy(
                src_ref=out_ref.at[side], dst_ref=in_ref.at[side],
                send_sem=ed_send.at[2 * which + side], recv_sem=ed_recv.at[2 * which + side],
                device_id=(g, lax.rem(s + step, sz.ns)), device_id_type=MESH,
            ).start()

    def wait_edges(ref, sems, which):
        for side in range(2):
            pltpu.make_async_copy(ref.at[side], ref.at[side], sems.at[2 * which + side]).wait()

    def start_fringe(out_ref, in_ref, which):
        in_ref[g] = out_ref[g]

        def send(p):
            pltpu.make_async_remote_copy(
                src_ref=out_ref.at[p], dst_ref=in_ref.at[g],
                send_sem=fr_send.at[which], recv_sem=fr_recv.at[which],
                device_id=(p, s), device_id_type=MESH,
            ).start()

        each_grid_peer(send)

    def wait_many(ref, number, sem):
        pltpu.make_async_copy(ref.at[pl.ds(0, number)], ref.at[pl.ds(0, number)], sem).wait()

    def own_terms(field_ref, out_ref):
        low_half = lane_ids((HALF, LANES)) < HALF
        for v in range(var_count):
            field = field_ref[v]
            flipped = swap_halves(field)
            left, right = jnp.where(low_half, field, flipped), jnp.where(low_half, flipped, field)
            for a in range(var_count):
                term = jeff_ref[1, a, v:v + 1, :] * left + jeff_ref[2, a, v:v + 1, :] * right
                base = field_ref[a] if v == 0 else out_ref[a]
                out_ref[a] = base + term

    def edge_terms(in_ref, out_ref):
        low_half = lane_ids((PACK, LANES)) < HALF
        for v in range(var_count):
            spread = []
            for side in range(2):
                packed = in_ref[side, v]
                flipped = swap_halves(packed)
                spread.append(jnp.concatenate(
                    [jnp.where(low_half, packed, flipped), jnp.where(low_half, flipped, packed)], axis=0))
            for a in range(var_count):
                term = jeff_ref[0, a, v:v + 1, :] * spread[0] + jeff_ref[3, a, v:v + 1, :] * spread[1]
                out_ref[a] = out_ref[a] + term

    def fringe_terms(in_ref, out_ref, chunk):
        left = []
        for k in range(len(chunk)):
            turned = jnp.transpose(in_ref[:, k, :])
            left.append(jnp.concatenate([turned[:HALF], turned[HALF:]], axis=1))
        lh, ll = halves(jnp.concatenate(left, axis=0))
        scatter = scatter_ref[...]
        total = dot1(lh, scatter, NN) + dot1(ll, scatter, NN)
        for k, v in enumerate(chunk):
            out_ref[v] = out_ref[v] + total[HALF * k:HALF * (k + 1)]

    loads["x"].wait()
    for k, chunk in enumerate(CHUNKS):
        fill_fringe(x_ref, send1[k], chunk)
        if k == 0:
            send1[0][:, len(chunk), :] = cell_row
            pl.semaphore_wait(barrier, sz.grid - 1 + sz.ns - 1)
        start_fringe(send1[k], got1[k], k)
    fill_edges(x_ref, edge_out1)
    start_edges(edge_out1, edge_in1, 0)

    loads["jac"].wait()
    loads["cols"].wait()
    side_on = [(s > 0).astype(F32), F32(1.0), F32(1.0), (s < sz.ns - 1).astype(F32)]
    listed = jac_ref.shape[3]
    low_lane = lane_ids((listed, LANES)) < HALF
    turn = row_ids((listed, LANES))
    picks = []
    for j in range(4):
        pick = jnp.zeros((listed, LANES), F32)
        for k in range(listed):
            left, right = [jnp.where(cols_ref[i, k] == j, side_on[j], F32(0.0)) for i in range(2)]
            pick = jnp.where(turn == k, jnp.where(low_lane, left, right), pick)
        picks.append(pick)
    for a in range(var_count):
        for b in range(var_count):
            both = jnp.concatenate([jac_ref[0, a, b], jac_ref[1, a, b]], axis=1)
            for j in range(4):
                jeff_ref[j, a, b:b + 1, :] = jnp.sum(picks[j] * both, axis=0, keepdims=True)

    own_terms(x_ref, w1_ref)
    wait_edges(edge_in1, ed_recv, 0)
    edge_terms(edge_in1, w1_ref)

    for k, chunk in enumerate(CHUNKS):
        wait_many(got1[k], sz.grid - 1, fr_recv.at[k])
        if k == 0:
            cells = got1[0][:, len(chunk), :]
            numbers = (lanes + 1).astype(F32)
            scatter_ref[...] = jnp.concatenate(
                [(cells[:, j * HALF:j * HALF + 1] == numbers).astype(F32) for j in range(2)], axis=0
            ).astype(BF16)
        fringe_terms(got1[k], w1_ref, chunk)
        fill_fringe(w1_ref, send2[k], chunk)
        start_fringe(send2[k], got2[k], count + k)
    fill_edges(w1_ref, edge_out2)
    start_edges(edge_out2, edge_in2, 1)

    def reduce_start(part, a_buf, which):
        mine = me1 * sz.share
        a_buf[me1] = part[pl.ds(mine, sz.share)]

        for column, slab in first_of:
            q = lax.div(column, sz.nc) * sz.ns + slab
            pltpu.make_async_remote_copy(
                src_ref=part.at[pl.ds(q * sz.share, sz.share)], dst_ref=a_buf.at[me1],
                send_sem=red_send.at[which], recv_sem=red_recv.at[which],
                device_id=(rows_of[-1] + column + core, slab), device_id_type=MESH,
            ).start()

    def reduce_middle(a_buf, mid, b_buf, which):
        wait_many(a_buf, sz.first - 1, red_recv.at[which])
        value = a_buf[0]
        for i in range(1, sz.first):
            value = value + a_buf[i]
        mid[...] = value
        b_buf[me2] = value

        for place in second_of:
            pltpu.make_async_remote_copy(
                src_ref=mid, dst_ref=b_buf.at[me2],
                send_sem=red_send.at[which + 1], recv_sem=red_recv.at[which + 1],
                device_id=(place + columns_of[-1], s), device_id_type=MESH,
            ).start()

    def reduce_last(b_buf, sum_buf, all_buf, which):
        wait_many(b_buf, sz.second - 1, red_recv.at[which + 1])
        value = b_buf[0]
        for i in range(1, sz.second):
            value = value + b_buf[i]
        sum_buf[...] = value
        all_buf[me1] = value

        for column, slab in first_of:
            pltpu.make_async_remote_copy(
                src_ref=sum_buf, dst_ref=all_buf.at[me1],
                send_sem=red_send.at[which + 2], recv_sem=red_recv.at[which + 2],
                device_id=(rows_of[-1] + column + core, slab), device_id_type=MESH,
            ).start()

    def reduced(all_buf, which):
        wait_many(all_buf, sz.first - 1, red_recv.at[which + 2])
        scale = 1.0 / sz.total_rows
        return [all_buf[:, :, t, :].reshape(PACK, LANES) * scale for t in range(3)]

    low_half = lane_ids((PACK, LANES)) < HALF
    wide_x = wide(x_ref)
    wide_1 = wide(w1_ref)
    pair = jnp.concatenate([wide_x, wide_1], axis=0)
    early = dot3(pair, pair, NT)
    part_e[:, 0, :] = early[:PACK]
    part_e[:, 1, :] = early[PACK:HALF]
    part_e[:, 2, :] = jnp.where(low_half, swap_halves(early[HALF:HALF + PACK]), early[HALF + PACK:])
    reduce_start(part_e, a_e, 0)
    own_terms(w1_ref, w2_ref)
    wait_edges(edge_in2, ed_recv, 1)
    edge_terms(edge_in2, w2_ref)
    for k, chunk in enumerate(CHUNKS):
        wait_many(got2[k], sz.grid - 1, fr_recv.at[count + k])
        fringe_terms(got2[k], w2_ref, chunk)

    wide_2 = wide(w2_ref)
    late = dot3(jnp.concatenate([wide_x, wide_1, wide_2], axis=0), wide_2, NT)
    for t in range(3):
        block = late[HALF * t:HALF * (t + 1)]
        part_l[:, t, :] = jnp.concatenate([block[:PACK], block[PACK:]], axis=1)
    reduce_start(part_l, a_l, 3)
    reduce_middle(a_e, mid_e, b_e, 0)
    reduce_middle(a_l, mid_l, b_l, 3)
    reduce_last(b_e, sum_e, all_e, 0)
    reduce_last(b_l, sum_l, all_l, 3)

    top, bottom, third = reduced(all_e, 0)
    own = jnp.concatenate([top[:, :HALF], bottom[:, :HALF]], axis=0)
    proj_1 = jnp.concatenate([top[:, HALF:], bottom[:, HALF:]], axis=0)
    twice_1 = 2.0 * proj_1 - dot3(own, proj_1, NN)
    gram_11 = split_rows(third) - dot3(proj_1, twice_1, TN)
    factor_11, inverse_11 = eliminate(gram_11)
    projected_1 = wide_1 - dot3(proj_1, wide_x, TN)
    basis_1 = dot3(inverse_11, projected_1, NN)
    for v in range(var_count):
        basis_ref[0, v] = basis_1[:, LANES * v:LANES * (v + 1)]

    proj_2, cross, square = [split_rows(value) for value in reduced(all_l, 3)]
    twice_2 = 2.0 * proj_2 - dot3(own, proj_2, NN)
    gram_12 = cross - dot3(twice_1, proj_2, TN)
    gram_22 = square - dot3(proj_2, twice_2, TN)
    factor_12 = dot3(inverse_11, gram_12, NN)
    factor_22, inverse_22 = eliminate(gram_22 - dot3(factor_12, factor_12, TN))
    projected_2 = wide_2 - dot3(proj_2, wide_x, TN) - dot3(factor_12, basis_1, TN)
    basis_2 = dot3(inverse_22, projected_2, NN)
    for v in range(var_count):
        basis_ref[1, v] = basis_2[:, LANES * v:LANES * (v + 1)]
    proj_ref[...] = jnp.concatenate([proj_1, proj_2], axis=1)
    factor_ref[...] = jnp.concatenate([
        jnp.concatenate([factor_11, factor_12], axis=1),
        jnp.concatenate([jnp.zeros((HALF, HALF), F32), factor_22], axis=1),
    ], axis=0)

    wait_edges(edge_out1, ed_send, 0)
    wait_edges(edge_out2, ed_send, 1)
    for k in range(count):
        wait_many(send1[k], sz.grid - 1, fr_send.at[k])
        wait_many(send2[k], sz.grid - 1, fr_send.at[count + k])
    for which, (a_buf, b_buf, all_buf) in ((0, (a_e, b_e, all_e)), (3, (a_l, b_l, all_l))):
        wait_many(a_buf, sz.first - 1, red_send.at[which])
        wait_many(b_buf, sz.second - 1, red_send.at[which + 1])
        wait_many(all_buf, sz.first - 1, red_send.at[which + 2])


def shards(sz, start_block, jacobian, block_cols, donor_cell, donor_weight, fringe_dest, recv_cell):
    var_count, rhs_count, cell_count = start_block.shape
    vmem = pl.BlockSpec(memory_space=pltpu.VMEM)
    field = (var_count, rhs_count, cell_count)
    edge = pltpu.VMEM((2, var_count, PACK, LANES), F32)
    sums = [
        pltpu.VMEM((PACK, 3, LANES), F32),
        pltpu.VMEM((sz.first, sz.share, 3, LANES), F32),
        pltpu.VMEM((sz.share, 3, LANES), F32),
        pltpu.VMEM((sz.second, sz.share, 3, LANES), F32),
        pltpu.VMEM((sz.share, 3, LANES), F32),
        pltpu.VMEM((sz.first, sz.share, 3, LANES), F32),
    ]
    inputs = (
        block_cols,
        start_block,
        jnp.transpose(jacobian, (0, 2, 3, 1, 4)),
        donor_cell.T,
        donor_weight.T,
        fringe_dest.reshape(1, -1),
        recv_cell.reshape(1, -1),
    )
    places = [pltpu.SMEM] + [pltpu.VMEM] * 6
    count = len(CHUNKS)
    first_chunks = [pltpu.VMEM((LANES, len(c) + (k == 0), LANES), F32) for k, c in enumerate(CHUNKS)]
    second_chunks = [pltpu.VMEM((LANES, len(c), LANES), F32) for c in CHUNKS]
    return pl.pallas_call(
        functools.partial(kernel, sz),
        out_shape=(
            jax.ShapeDtypeStruct((2,) + field, F32),
            jax.ShapeDtypeStruct((rhs_count, 2 * rhs_count), F32),
            jax.ShapeDtypeStruct((2 * rhs_count, 2 * rhs_count), F32),
        ),
        in_specs=[pl.BlockSpec(memory_space=HBM)] * 7,
        out_specs=(vmem, vmem, vmem),
        scratch_shapes=[
            *[place(value.shape, value.dtype) for place, value in zip(places, inputs)],
            pltpu.SemaphoreType.DMA((7,)),
            pltpu.VMEM(field, F32),
            pltpu.VMEM(field, F32),
            pltpu.VMEM((4, var_count, 8, LANES), F32),
            pltpu.VMEM((LANES, 2 * LANES), BF16),
            pltpu.VMEM((LANES, 2 * LANES), BF16),
            pltpu.VMEM((2 * LANES, LANES), BF16),
            edge, edge, edge, edge,
            *sums, *sums,
            pltpu.SemaphoreType.DMA((2 * count,)),
            pltpu.SemaphoreType.DMA((2 * count,)),
            pltpu.SemaphoreType.DMA((4,)),
            pltpu.SemaphoreType.DMA((4,)),
            pltpu.SemaphoreType.DMA((6,)),
            pltpu.SemaphoreType.DMA((6,)),
            *first_chunks, *first_chunks, *second_chunks, *second_chunks,
        ],
        compiler_params=pltpu.CompilerParams(
            collective_id=0, has_side_effects=True, vmem_limit_bytes=32 * 1024 * 1024
        ),
    )(*[pltpu.with_memory_space_constraint(value, HBM) for value in inputs])


def solution(mesh):
    grid, slab = mesh.shape["grid"], mesh.shape["slab"]
    side = 8 if grid == 128 else 1
    sz = Sizes(grid // (2 * side), side, 2, slab, 5 * 128 * grid * slab)
    both = ("grid", "slab")
    in_specs = (
        P(None, None, both),
        P(both, None, None, None, None),
        P(both, None),
        P(both, None),
        P(both, None),
        P(both, None),
        P(both),
    )
    out_specs = (P(None, None, None, both), P(), P())
    return jax.shard_map(
        functools.partial(shards, sz), mesh=mesh, in_specs=in_specs, out_specs=out_specs, check_vma=False
    )
```

```python
import functools

import jax
import jax.numpy as jnp
from jax import lax
from jax.experimental import pallas as pl
from jax.experimental.pallas import tpu as pltpu
from jax.sharding import PartitionSpec as P

MESH = pl.DeviceIdType.MESH
F32 = jnp.float32
BF16 = jnp.bfloat16
NT = (((1,), (1,)), ((), ()))
NN = (((1,), (0,)), ((), ()))
TN = (((0,), (0,)), ((), ()))
LANES = 128
HALF = 64
PACK = 32
HBM = pltpu.HBM


def halves(x):
    high = x.astype(BF16)
    return high, (x - high.astype(F32)).astype(BF16)


def dot1(a, b, dims):
    return lax.dot_general(a, b, dims, preferred_element_type=F32)


def dot3(a, b, dims):
    ah, al = halves(a)
    bh, bl = halves(b)
    return dot1(ah, bh, dims) + (dot1(ah, bl, dims) + dot1(al, bh, dims))


def lane_ids(shape):
    return lax.broadcasted_iota(jnp.int32, shape, len(shape) - 1)


def row_ids(shape):
    return lax.broadcasted_iota(jnp.int32, shape, len(shape) - 2)


def swap_halves(x):
    return pltpu.roll(x, HALF, x.ndim - 1)


def wide(field):
    return jnp.concatenate([field[v] for v in range(field.shape[0])], axis=1)


def split_rows(packed):
    return jnp.concatenate([packed[:, :HALF], packed[:, HALF:]], axis=0)


def eliminate(gram):
    size = gram.shape[0]
    eye = (row_ids((size, size)) == lane_ids((size, size))).astype(F32)
    work = jnp.concatenate([gram, eye], axis=1)
    blocks = [work[8 * i:8 * i + 8] for i in range(size // 8)]
    sub = row_ids((8, LANES))
    done = []
    for kb in range(len(blocks)):
        cols = {
            i: [jnp.broadcast_to(blocks[i][:, 8 * kb + t:8 * kb + t + 1], (8, LANES)) for t in range(8)]
            for i in range(kb, len(blocks))
        }
        pivots = jnp.ones((8, LANES), F32)
        for t in range(8):
            row = jnp.broadcast_to(blocks[kb][t:t + 1], (8, LANES))
            heads = [jnp.broadcast_to(cols[kb][u][t:t + 1], (8, LANES)) for u in range(t, 8)]
            inverse = 1.0 / heads[0]
            pivots = jnp.where(sub == t, heads[0], pivots)
            for i in range(kb, len(blocks)):
                ratio = cols[i][t] * inverse
                if i == kb:
                    ratio = jnp.where(sub > t, ratio, 0.0)
                for u in range(t + 1, 8):
                    cols[i][u] = cols[i][u] - ratio * heads[u - t]
                blocks[i] = blocks[i] - ratio * row
        done.append(blocks[kb] * lax.rsqrt(pivots))
    both = jnp.concatenate(done, axis=0)
    upper = jnp.where(row_ids((size, size)) <= lane_ids((size, size)), both[:, :size], 0.0)
    return upper, both[:, size:]


class Sizes:
    def __init__(self, ny, nz, nc, ns, total_rows):
        self.ny, self.nz, self.nc, self.ns = ny, nz, nc, ns
        self.grid = ny * nz * nc
        self.first, self.second = nz * ns, ny * nc
        self.share = PACK // self.first
        self.total_rows = total_rows


CHUNKS = ((0,), (1, 2), (3, 4))


def ring(size):
    return sorted(range(size), key=lambda step: -min(step, size - step))


def kernel(sz, *refs):
    (cols_hbm, x_hbm, jac_hbm, cell_hbm, weight_hbm, dest_hbm, recv_hbm,
     basis_ref, proj_ref, factor_ref,
     cols_ref, x_ref, jac_ref, cell_ref, weight_ref, dest_ref, recv_ref, load_sem,
     v_ref, u_ref, jeff_ref, place_high, place_low, scatter_ref,
     edge_out1, edge_in1, edge_out2, edge_in2,
     part_e, a_e, mid_e, b_e, sum_e, all_e,
     part_l, a_l, mid_l, b_l, sum_l, all_l,
     fr_send, fr_recv, ed_send, ed_recv, red_send, red_recv, *fringe) = refs
    count = len(CHUNKS)
    send1, got1, send2, got2 = [fringe[k * count:(k + 1) * count] for k in range(4)]
    var_count = x_ref.shape[0]
    g = lax.axis_index("grid")
    s = lax.axis_index("slab")
    core = lax.rem(g, sz.nc)
    z = lax.rem(lax.div(g, sz.nc), sz.nz)
    y = lax.div(g, sz.nc * sz.nz)
    me1 = z * sz.ns + s
    me2 = y * sz.nc + core

    rows_of = [lax.rem(y + step, sz.ny) * (sz.nz * sz.nc) for step in ring(sz.ny)]
    columns_of = [lax.rem(z + step, sz.nz) * sz.nc for step in ring(sz.nz)]
    cores_of = [lax.rem(core + step, sz.nc) for step in ring(sz.nc)]
    slabs_of = [lax.rem(s + step, sz.ns) for step in ring(sz.ns)]
    plane_of = [column + part for column in columns_of for part in cores_of]
    first_of = [(column, slab) for column in columns_of for slab in slabs_of][:-1]
    second_of = [row + part for row in rows_of for part in cores_of][:-1]

    def each_grid_peer(act):
        def body(i, carry):
            row = lax.rem(y + sz.ny // 2 + lax.div(i + 1, 2) * (1 - 2 * lax.rem(i, 2)), sz.ny) * (sz.nz * sz.nc)
            for place in plane_of:
                act(row + place)
            return carry

        lax.fori_loop(0, sz.ny - 1, body, 0)
        for place in plane_of[:-1]:
            act(rows_of[-1] + place)

    if sz.grid < LANES:
        for ref in (*got1, *got2):
            ref[...] = jnp.zeros_like(ref)

    barrier = pltpu.get_barrier_semaphore()

    def greet(p):
        pl.semaphore_signal(barrier, inc=1, device_id=(p, s), device_id_type=MESH)

    each_grid_peer(greet)
    for step in range(1, sz.ns):
        pl.semaphore_signal(barrier, inc=1, device_id=(g, lax.rem(s + step, sz.ns)), device_id_type=MESH)

    loads = {}
    for k, (name, source, target) in enumerate((
        ("dest", dest_hbm, dest_ref), ("cell", cell_hbm, cell_ref), ("weight", weight_hbm, weight_ref),
        ("recv", recv_hbm, recv_ref), ("x", x_hbm, x_ref), ("jac", jac_hbm, jac_ref), ("cols", cols_hbm, cols_ref),
    )):
        loads[name] = pltpu.make_async_copy(source, target, load_sem.at[k])
        loads[name].start()

    rows = dest_ref.shape[1]
    ids = row_ids((LANES, rows))
    for name in ("dest", "cell", "weight", "recv"):
        loads[name].wait()
    named = dest_ref[...] == ids
    later = (row_ids((rows, rows)) < lane_ids((rows, rows))).astype(BF16)
    rank = dot1(named.astype(BF16), later, NN)
    slots = jnp.concatenate(
        [jnp.where(named, (rank == float(j)).astype(F32), 0.0) for j in range(2)], axis=0
    ).astype(BF16)
    weight_mat = jnp.zeros((LANES, rows), F32)
    for t in range(cell_ref.shape[0]):
        weight_mat += jnp.where(cell_ref[t:t + 1, :] == ids, weight_ref[t:t + 1, :], 0.0)
    numbers = jnp.broadcast_to(recv_ref[...].astype(F32) + 1.0, (LANES, rows))
    th, tl = halves(jnp.concatenate([weight_mat, numbers], axis=0))
    placed = dot1(slots, th, NT) + dot1(slots, tl, NT)
    place_high[...], place_low[...] = halves(
        jnp.concatenate([placed[:LANES, :LANES], placed[LANES:, :LANES]], axis=1))
    lanes = lane_ids((LANES, LANES))
    cell_row = jnp.where(lanes < HALF, placed[:LANES, LANES:], placed[LANES:, LANES:])

    def fill_fringe(field_ref, out_ref, chunk):
        zero = jnp.zeros((HALF, LANES), F32)
        blocks = []
        for v in chunk:
            field = field_ref[v]
            blocks += [jnp.concatenate([field, zero], axis=1), jnp.concatenate([zero, field], axis=1)]
        fh, fl = halves(jnp.concatenate(blocks, axis=0))
        ph, plow = place_high[...], place_low[...]
        out = dot1(ph, fh, NT) + (dot1(ph, fl, NT) + dot1(plow, fh, NT))
        for k in range(len(chunk)):
            out_ref[:, k, :] = out[:, LANES * k:LANES * (k + 1)]

    def fill_edges(field_ref, out_ref):
        low_half = lane_ids((PACK, LANES)) < HALF
        for v in range(var_count):
            top, bottom = field_ref[v, :PACK, :], field_ref[v, PACK:, :]
            out_ref[0, v] = jnp.where(low_half, swap_halves(top), bottom)
            out_ref[1, v] = jnp.where(low_half, top, swap_halves(bottom))

    def start_edges(out_ref, in_ref, which):
        for side, step in ((0, 1), (1, sz.ns - 1)):
            pltpu.make_async_remote_copy(
                src_ref=out_ref.at[side], dst_ref=in_ref.at[side],
                send_sem=ed_send.at[2 * which + side], recv_sem=ed_recv.at[2 * which + side],
                device_id=(g, lax.rem(s + step, sz.ns)), device_id_type=MESH,
            ).start()

    def wait_edges(ref, sems, which):
        for side in range(2):
            pltpu.make_async_copy(ref.at[side], ref.at[side], sems.at[2 * which + side]).wait()

    def start_fringe(out_ref, in_ref, which):
        in_ref[g] = out_ref[g]

        def send(p):
            pltpu.make_async_remote_copy(
                src_ref=out_ref.at[p], dst_ref=in_ref.at[g],
                send_sem=fr_send.at[which], recv_sem=fr_recv.at[which],
                device_id=(p, s), device_id_type=MESH,
            ).start()

        each_grid_peer(send)

    def wait_many(ref, number, sem):
        pltpu.make_async_copy(ref.at[pl.ds(0, number)], ref.at[pl.ds(0, number)], sem).wait()

    def own_terms(field_ref, out_ref):
        low_half = lane_ids((HALF, LANES)) < HALF
        for v in range(var_count):
            field = field_ref[v]
            flipped = swap_halves(field)
            left, right = jnp.where(low_half, field, flipped), jnp.where(low_half, flipped, field)
            for a in range(var_count):
                term = jeff_ref[1, a, v:v + 1, :] * left + jeff_ref[2, a, v:v + 1, :] * right
                out_ref[a] = term if v == 0 else out_ref[a] + term

    def edge_terms(in_ref, out_ref):
        low_half = lane_ids((PACK, LANES)) < HALF
        for v in range(var_count):
            spread = []
            for side in range(2):
                packed = in_ref[side, v]
                flipped = swap_halves(packed)
                spread.append(jnp.concatenate(
                    [jnp.where(low_half, packed, flipped), jnp.where(low_half, flipped, packed)], axis=0))
            for a in range(var_count):
                term = jeff_ref[0, a, v:v + 1, :] * spread[0] + jeff_ref[3, a, v:v + 1, :] * spread[1]
                out_ref[a] = out_ref[a] + term

    def fringe_terms(in_ref, out_ref, chunk):
        left = []
        for k in range(len(chunk)):
            turned = jnp.transpose(in_ref[:, k, :])
            left.append(jnp.concatenate([turned[:HALF], turned[HALF:]], axis=1))
        lh, ll = halves(jnp.concatenate(left, axis=0))
        scatter = scatter_ref[...]
        total = dot1(lh, scatter, NN) + dot1(ll, scatter, NN)
        for k, v in enumerate(chunk):
            out_ref[v] = out_ref[v] + total[HALF * k:HALF * (k + 1)]

    loads["x"].wait()
    for k, chunk in enumerate(CHUNKS):
        fill_fringe(x_ref, send1[k], chunk)
    send1[0][:, len(CHUNKS[0]), :] = cell_row
    fill_edges(x_ref, edge_out1)
    pl.semaphore_wait(barrier, sz.grid - 1 + sz.ns - 1)
    for k in range(count):
        start_fringe(send1[k], got1[k], k)
    start_edges(edge_out1, edge_in1, 0)

    loads["jac"].wait()
    loads["cols"].wait()
    side_on = [(s > 0).astype(F32), F32(1.0), F32(1.0), (s < sz.ns - 1).astype(F32)]
    listed = jac_ref.shape[3]
    low_lane = lane_ids((listed, LANES)) < HALF
    turn = row_ids((listed, LANES))
    picks = []
    for j in range(4):
        pick = jnp.zeros((listed, LANES), F32)
        for k in range(listed):
            left, right = [jnp.where(cols_ref[i, k] == j, side_on[j], F32(0.0)) for i in range(2)]
            pick = jnp.where(turn == k, jnp.where(low_lane, left, right), pick)
        picks.append(pick)
    for a in range(var_count):
        for b in range(var_count):
            both = jnp.concatenate([jac_ref[0, a, b], jac_ref[1, a, b]], axis=1)
            for j in range(4):
                jeff_ref[j, a, b:b + 1, :] = jnp.sum(picks[j] * both, axis=0, keepdims=True)

    own_terms(x_ref, v_ref)
    wait_edges(edge_in1, ed_recv, 0)
    edge_terms(edge_in1, v_ref)

    for k, chunk in enumerate(CHUNKS):
        wait_many(got1[k], sz.grid - 1, fr_recv.at[k])
        if k == 0:
            cells = got1[0][:, len(chunk), :]
            numbers = (lanes + 1).astype(F32)
            scatter_ref[...] = jnp.concatenate(
                [(cells[:, j * HALF:j * HALF + 1] == numbers).astype(F32) for j in range(2)], axis=0
            ).astype(BF16)
        fringe_terms(got1[k], v_ref, chunk)
        fill_fringe(v_ref, send2[k], chunk)
        start_fringe(send2[k], got2[k], count + k)
    fill_edges(v_ref, edge_out2)
    start_edges(edge_out2, edge_in2, 1)

    def reduce_start(part, a_buf, which):
        mine = me1 * sz.share
        a_buf[me1] = part[pl.ds(mine, sz.share)]

        for column, slab in first_of:
            q = lax.div(column, sz.nc) * sz.ns + slab
            pltpu.make_async_remote_copy(
                src_ref=part.at[pl.ds(q * sz.share, sz.share)], dst_ref=a_buf.at[me1],
                send_sem=red_send.at[which], recv_sem=red_recv.at[which],
                device_id=(rows_of[-1] + column + core, slab), device_id_type=MESH,
            ).start()

    def reduce_middle(a_buf, mid, b_buf, which):
        wait_many(a_buf, sz.first - 1, red_recv.at[which])
        value = a_buf[0]
        for i in range(1, sz.first):
            value = value + a_buf[i]
        mid[...] = value
        b_buf[me2] = value

        for place in second_of:
            pltpu.make_async_remote_copy(
                src_ref=mid, dst_ref=b_buf.at[me2],
                send_sem=red_send.at[which + 1], recv_sem=red_recv.at[which + 1],
                device_id=(place + columns_of[-1], s), device_id_type=MESH,
            ).start()

    def reduce_last(b_buf, sum_buf, all_buf, which):
        wait_many(b_buf, sz.second - 1, red_recv.at[which + 1])
        value = b_buf[0]
        for i in range(1, sz.second):
            value = value + b_buf[i]
        sum_buf[...] = value
        all_buf[me1] = value

        for column, slab in first_of:
            pltpu.make_async_remote_copy(
                src_ref=sum_buf, dst_ref=all_buf.at[me1],
                send_sem=red_send.at[which + 2], recv_sem=red_recv.at[which + 2],
                device_id=(rows_of[-1] + column + core, slab), device_id_type=MESH,
            ).start()

    def reduced(all_buf, which):
        wait_many(all_buf, sz.first - 1, red_recv.at[which + 2])
        scale = 1.0 / sz.total_rows
        return [all_buf[:, :, t, :].reshape(PACK, LANES) * scale for t in range(3)]

    low_half = lane_ids((PACK, LANES)) < HALF
    wide_x = wide(x_ref)
    wide_v = wide(v_ref)
    pair = jnp.concatenate([wide_x, wide_v], axis=0)
    early = dot3(pair, pair, NT)
    part_e[:, 0, :] = early[:PACK]
    part_e[:, 1, :] = early[PACK:HALF]
    part_e[:, 2, :] = jnp.where(low_half, swap_halves(early[HALF:HALF + PACK]), early[HALF + PACK:])
    reduce_start(part_e, a_e, 0)
    own_terms(v_ref, u_ref)
    wait_edges(edge_in2, ed_recv, 1)
    edge_terms(edge_in2, u_ref)
    late = jnp.zeros((3 * HALF, HALF), F32)
    for k, chunk in enumerate(CHUNKS):
        wait_many(got2[k], sz.grid - 1, fr_recv.at[count + k])
        fringe_terms(got2[k], u_ref, chunk)
        parts = [jnp.concatenate([ref[v] for v in chunk], axis=1) for ref in (x_ref, v_ref, u_ref)]
        late = late + dot3(jnp.concatenate(parts, axis=0), parts[2], NT)
    for t in range(3):
        block = late[HALF * t:HALF * (t + 1)]
        part_l[:, t, :] = jnp.concatenate([block[:PACK], block[PACK:]], axis=1)
    reduce_start(part_l, a_l, 3)
    reduce_middle(a_e, mid_e, b_e, 0)
    reduce_middle(a_l, mid_l, b_l, 3)
    reduce_last(b_e, sum_e, all_e, 0)
    reduce_last(b_l, sum_l, all_l, 3)

    top, bottom, third = reduced(all_e, 0)
    own = jnp.concatenate([top[:, :HALF], bottom[:, :HALF]], axis=0)
    with_v = jnp.concatenate([top[:, HALF:], bottom[:, HALF:]], axis=0)
    eye = (row_ids((HALF, HALF)) == lane_ids((HALF, HALF))).astype(F32)
    proj_1 = own + with_v
    lack_1 = eye - proj_1
    left_1 = with_v + dot3(own, lack_1, NN)
    gram_11 = split_rows(third) + dot3(
        jnp.concatenate([with_v, lack_1], axis=0), jnp.concatenate([lack_1, left_1], axis=0), TN)
    factor_11, inverse_11 = eliminate(gram_11)
    wide_u = wide(u_ref)
    basis_1 = dot3(inverse_11, wide_v + dot3(lack_1, wide_x, TN), NN)
    for v in range(var_count):
        basis_ref[0, v] = basis_1[:, LANES * v:LANES * (v + 1)]
    solver = jnp.concatenate(
        [inverse_11, dot3(inverse_11, left_1, NT), dot3(inverse_11, lack_1, NT)], axis=1)

    with_u, cross, square = [split_rows(value) for value in reduced(all_l, 3)]
    lack_3 = (own - eye) - with_u
    left_3 = with_u + dot3(own, lack_3, NN)
    factor_13 = dot3(solver, jnp.concatenate([cross, lack_3, with_u], axis=0), NN)
    gram_33 = square + dot3(
        jnp.concatenate([with_u, lack_3], axis=0), jnp.concatenate([lack_3, left_3], axis=0), TN)
    factor_22, inverse_22 = eliminate(gram_33 - dot3(factor_13, factor_13, TN))
    rest = wide_u + dot3(
        jnp.concatenate([lack_3, -factor_13], axis=0), jnp.concatenate([wide_x, basis_1], axis=0), TN)
    basis_2 = dot3(inverse_22, rest, NN)
    for v in range(var_count):
        basis_ref[1, v] = basis_2[:, LANES * v:LANES * (v + 1)]
    proj_ref[...] = jnp.concatenate([proj_1, (proj_1 + with_v) + with_u], axis=1)
    factor_ref[...] = jnp.concatenate([
        jnp.concatenate([factor_11, 2.0 * factor_11 + factor_13], axis=1),
        jnp.concatenate([jnp.zeros((HALF, HALF), F32), factor_22], axis=1),
    ], axis=0)

    wait_edges(edge_out1, ed_send, 0)
    wait_edges(edge_out2, ed_send, 1)
    for k in range(count):
        wait_many(send1[k], sz.grid - 1, fr_send.at[k])
        wait_many(send2[k], sz.grid - 1, fr_send.at[count + k])
    for which, (a_buf, b_buf, all_buf) in ((0, (a_e, b_e, all_e)), (3, (a_l, b_l, all_l))):
        wait_many(a_buf, sz.first - 1, red_send.at[which])
        wait_many(b_buf, sz.second - 1, red_send.at[which + 1])
        wait_many(all_buf, sz.first - 1, red_send.at[which + 2])


def write_out(basis_ref, proj_ref, factor_ref, basis_hbm, proj_hbm, factor_hbm, sems):
    pairs = ((basis_ref, basis_hbm), (proj_ref, proj_hbm), (factor_ref, factor_hbm))
    copies = [pltpu.make_async_copy(source, target, sems.at[k]) for k, (source, target) in enumerate(pairs)]
    for copy in copies:
        copy.start()
    for copy in copies:
        copy.wait()


def shards(sz, start_block, jacobian, block_cols, donor_cell, donor_weight, fringe_dest, recv_cell):
    var_count, rhs_count, cell_count = start_block.shape
    vmem = pl.BlockSpec(memory_space=pltpu.VMEM)
    field = (var_count, rhs_count, cell_count)
    edge = pltpu.VMEM((2, var_count, PACK, LANES), F32)
    sums = [
        pltpu.VMEM((PACK, 3, LANES), F32),
        pltpu.VMEM((sz.first, sz.share, 3, LANES), F32),
        pltpu.VMEM((sz.share, 3, LANES), F32),
        pltpu.VMEM((sz.second, sz.share, 3, LANES), F32),
        pltpu.VMEM((sz.share, 3, LANES), F32),
        pltpu.VMEM((sz.first, sz.share, 3, LANES), F32),
    ]
    inputs = (
        block_cols,
        start_block,
        jnp.transpose(jacobian, (0, 2, 3, 1, 4)),
        donor_cell.T,
        donor_weight.T,
        fringe_dest.reshape(1, -1),
        recv_cell.reshape(1, -1),
    )
    places = [pltpu.SMEM] + [pltpu.VMEM] * 6
    count = len(CHUNKS)
    first_chunks = [pltpu.VMEM((LANES, len(c) + (k == 0), LANES), F32) for k, c in enumerate(CHUNKS)]
    second_chunks = [pltpu.VMEM((LANES, len(c), LANES), F32) for c in CHUNKS]
    results = pl.pallas_call(
        functools.partial(kernel, sz),
        out_shape=(
            jax.ShapeDtypeStruct((2,) + field, F32),
            jax.ShapeDtypeStruct((rhs_count, 2 * rhs_count), F32),
            jax.ShapeDtypeStruct((2 * rhs_count, 2 * rhs_count), F32),
        ),
        in_specs=[pl.BlockSpec(memory_space=HBM)] * 7,
        out_specs=(vmem, vmem, vmem),
        scratch_shapes=[
            *[place(value.shape, value.dtype) for place, value in zip(places, inputs)],
            pltpu.SemaphoreType.DMA((7,)),
            pltpu.VMEM(field, F32),
            pltpu.VMEM(field, F32),
            pltpu.VMEM((4, var_count, 8, LANES), F32),
            pltpu.VMEM((LANES, 2 * LANES), BF16),
            pltpu.VMEM((LANES, 2 * LANES), BF16),
            pltpu.VMEM((2 * LANES, LANES), BF16),
            edge, edge, edge, edge,
            *sums, *sums,
            pltpu.SemaphoreType.DMA((2 * count,)),
            pltpu.SemaphoreType.DMA((2 * count,)),
            pltpu.SemaphoreType.DMA((4,)),
            pltpu.SemaphoreType.DMA((4,)),
            pltpu.SemaphoreType.DMA((6,)),
            pltpu.SemaphoreType.DMA((6,)),
            *first_chunks, *first_chunks, *second_chunks, *second_chunks,
        ],
        compiler_params=pltpu.CompilerParams(
            collective_id=0, has_side_effects=True, vmem_limit_bytes=32 * 1024 * 1024
        ),
    )(*[pltpu.with_memory_space_constraint(value, HBM) for value in inputs])
    return pl.pallas_call(
        write_out,
        out_shape=tuple(jax.ShapeDtypeStruct(value.shape, value.dtype) for value in results),
        in_specs=[vmem] * 3,
        out_specs=(pl.BlockSpec(memory_space=HBM),) * 3,
        scratch_shapes=[pltpu.SemaphoreType.DMA((3,))],
    )(*results)


def solution(mesh):
    grid, slab = mesh.shape["grid"], mesh.shape["slab"]
    side = 8 if grid == 128 else 1
    sz = Sizes(grid // (2 * side), side, 2, slab, 5 * 128 * grid * slab)
    both = ("grid", "slab")
    in_specs = (
        P(None, None, both),
        P(both, None, None, None, None),
        P(both, None),
        P(both, None),
        P(both, None),
        P(both, None),
        P(both),
    )
    out_specs = (P(None, None, None, both), P(), P())
    return jax.shard_map(
        functools.partial(shards, sz), mesh=mesh, in_specs=in_specs, out_specs=out_specs, check_vma=False
    )
```

```python
import functools

import jax
import jax.numpy as jnp
from jax import lax
from jax.experimental import pallas as pl
from jax.experimental.pallas import tpu as pltpu
from jax.sharding import PartitionSpec as P

MESH = pl.DeviceIdType.MESH
F32 = jnp.float32
BF16 = jnp.bfloat16
NT = (((1,), (1,)), ((), ()))
NN = (((1,), (0,)), ((), ()))
TN = (((0,), (0,)), ((), ()))
LANES = 128
HALF = 64
PACK = 32
HBM = pltpu.HBM


def halves(x):
    high = x.astype(BF16)
    return high, (x - high.astype(F32)).astype(BF16)


def dot1(a, b, dims):
    return lax.dot_general(a, b, dims, preferred_element_type=F32)


def dot3(a, b, dims):
    ah, al = halves(a)
    bh, bl = halves(b)
    return dot1(ah, bh, dims) + (dot1(ah, bl, dims) + dot1(al, bh, dims))


def lane_ids(shape):
    return lax.broadcasted_iota(jnp.int32, shape, len(shape) - 1)


def row_ids(shape):
    return lax.broadcasted_iota(jnp.int32, shape, len(shape) - 2)


def swap_halves(x):
    return pltpu.roll(x, HALF, x.ndim - 1)


def wide(field):
    return jnp.concatenate([field[v] for v in range(field.shape[0])], axis=1)


def split_rows(packed):
    return jnp.concatenate([packed[:, :HALF], packed[:, HALF:]], axis=0)


def eliminate(gram):
    size = gram.shape[0]
    eye = (row_ids((size, size)) == lane_ids((size, size))).astype(F32)
    work = jnp.concatenate([gram, eye], axis=1)
    blocks = [work[8 * i:8 * i + 8] for i in range(size // 8)]
    sub = row_ids((8, LANES))
    done = []
    for kb in range(len(blocks)):
        cols = {
            i: [jnp.broadcast_to(blocks[i][:, 8 * kb + t:8 * kb + t + 1], (8, LANES)) for t in range(8)]
            for i in range(kb, len(blocks))
        }
        pivots = jnp.ones((8, LANES), F32)
        for t in range(8):
            row = jnp.broadcast_to(blocks[kb][t:t + 1], (8, LANES))
            heads = [jnp.broadcast_to(cols[kb][u][t:t + 1], (8, LANES)) for u in range(t, 8)]
            inverse = 1.0 / heads[0]
            pivots = jnp.where(sub == t, heads[0], pivots)
            for i in range(kb, len(blocks)):
                ratio = cols[i][t] * inverse
                if i == kb:
                    ratio = jnp.where(sub > t, ratio, 0.0)
                for u in range(t + 1, 8):
                    cols[i][u] = cols[i][u] - ratio * heads[u - t]
                blocks[i] = blocks[i] - ratio * row
        done.append(blocks[kb] * lax.rsqrt(pivots))
    both = jnp.concatenate(done, axis=0)
    upper = jnp.where(row_ids((size, size)) <= lane_ids((size, size)), both[:, :size], 0.0)
    return upper, both[:, size:]


class Sizes:
    def __init__(self, ny, nz, nc, ns, total_rows):
        self.ny, self.nz, self.nc, self.ns = ny, nz, nc, ns
        self.grid = ny * nz * nc
        self.first, self.second = nz * ns, ny * nc
        self.share = PACK // self.first
        self.total_rows = total_rows


CHUNKS = ((0,), (1, 2), (3, 4))


def ring(size):
    return sorted(range(size), key=lambda step: -min(step, size - step))


def kernel(sz, *refs):
    (cols_hbm, x_hbm, jac_hbm, cell_hbm, weight_hbm, dest_hbm, recv_hbm,
     basis_ref, proj_ref, factor_ref,
     cols_ref, x_ref, jac_ref, cell_ref, weight_ref, dest_ref, recv_ref, load_sem,
     v_ref, u_ref, jeff_ref, place_high, place_low, scatter_ref,
     edge_out1, edge_in1, edge_out2, edge_in2,
     part_e, a_e, mid_e, b_e, sum_e, all_e,
     part_l, a_l, mid_l, b_l, sum_l, all_l,
     fr_send, fr_recv, ed_send, ed_recv, red_send, red_recv, *fringe) = refs
    count = len(CHUNKS)
    send1, got1, send2, got2 = [fringe[k * count:(k + 1) * count] for k in range(4)]
    var_count = x_ref.shape[0]
    g = lax.axis_index("grid")
    s = lax.axis_index("slab")
    core = lax.rem(g, sz.nc)
    z = lax.rem(lax.div(g, sz.nc), sz.nz)
    y = lax.div(g, sz.nc * sz.nz)
    me1 = z * sz.ns + s
    me2 = y * sz.nc + core

    rows_of = [lax.rem(y + step, sz.ny) * (sz.nz * sz.nc) for step in ring(sz.ny)]
    columns_of = [lax.rem(z + step, sz.nz) * sz.nc for step in ring(sz.nz)]
    cores_of = [lax.rem(core + step, sz.nc) for step in ring(sz.nc)]
    slabs_of = [lax.rem(s + step, sz.ns) for step in ring(sz.ns)]
    plane_of = [column + part for column in columns_of for part in cores_of]
    first_of = [(column, slab) for column in columns_of for slab in slabs_of][:-1]
    second_of = [row + part for row in rows_of for part in cores_of][:-1]

    def each_grid_peer(act):
        def body(i, carry):
            row = lax.rem(y + sz.ny // 2 + lax.div(i + 1, 2) * (1 - 2 * lax.rem(i, 2)), sz.ny) * (sz.nz * sz.nc)
            for place in plane_of:
                act(row + place)
            return carry

        lax.fori_loop(0, sz.ny - 1, body, 0)
        for place in plane_of[:-1]:
            act(rows_of[-1] + place)

    if sz.grid < LANES:
        for ref in (*got1, *got2):
            ref[...] = jnp.zeros_like(ref)

    barrier = pltpu.get_barrier_semaphore()

    def greet(p):
        pl.semaphore_signal(barrier, inc=1, device_id=(p, s), device_id_type=MESH)

    each_grid_peer(greet)
    for step in range(1, sz.ns):
        pl.semaphore_signal(barrier, inc=1, device_id=(g, lax.rem(s + step, sz.ns)), device_id_type=MESH)

    loads = {}
    for k, (name, source, target) in enumerate((
        ("dest", dest_hbm, dest_ref), ("cell", cell_hbm, cell_ref), ("weight", weight_hbm, weight_ref),
        ("recv", recv_hbm, recv_ref), ("x", x_hbm, x_ref), ("jac", jac_hbm, jac_ref), ("cols", cols_hbm, cols_ref),
    )):
        loads[name] = pltpu.make_async_copy(source, target, load_sem.at[k])
        loads[name].start()

    rows = dest_ref.shape[1]
    ids = row_ids((LANES, rows))
    for name in ("dest", "cell", "weight", "recv"):
        loads[name].wait()
    named = dest_ref[...] == ids
    later = (row_ids((rows, rows)) < lane_ids((rows, rows))).astype(BF16)
    rank = dot1(named.astype(BF16), later, NN)
    slots = jnp.concatenate(
        [jnp.where(named, (rank == float(j)).astype(F32), 0.0) for j in range(2)], axis=0
    ).astype(BF16)
    weight_mat = jnp.zeros((LANES, rows), F32)
    for t in range(cell_ref.shape[0]):
        weight_mat += jnp.where(cell_ref[t:t + 1, :] == ids, weight_ref[t:t + 1, :], 0.0)
    numbers = jnp.broadcast_to(recv_ref[...].astype(F32) + 1.0, (LANES, rows))
    th, tl = halves(jnp.concatenate([weight_mat, numbers], axis=0))
    placed = dot1(slots, th, NT) + dot1(slots, tl, NT)
    place_high[...], place_low[...] = halves(
        jnp.concatenate([placed[:LANES, :LANES], placed[LANES:, :LANES]], axis=1))
    lanes = lane_ids((LANES, LANES))
    cell_row = jnp.where(lanes < HALF, placed[:LANES, LANES:], placed[LANES:, LANES:])

    def fill_fringe(field_ref, out_ref, chunk):
        zero = jnp.zeros((HALF, LANES), F32)
        blocks = []
        for v in chunk:
            field = field_ref[v]
            blocks += [jnp.concatenate([field, zero], axis=1), jnp.concatenate([zero, field], axis=1)]
        fh, fl = halves(jnp.concatenate(blocks, axis=0))
        ph, plow = place_high[...], place_low[...]
        out = dot1(ph, fh, NT) + (dot1(ph, fl, NT) + dot1(plow, fh, NT))
        for k in range(len(chunk)):
            out_ref[:, k, :] = out[:, LANES * k:LANES * (k + 1)]

    def fill_edges(field_ref, out_ref):
        low_half = lane_ids((PACK, LANES)) < HALF
        for v in range(var_count):
            top, bottom = field_ref[v, :PACK, :], field_ref[v, PACK:, :]
            out_ref[0, v] = jnp.where(low_half, swap_halves(top), bottom)
            out_ref[1, v] = jnp.where(low_half, top, swap_halves(bottom))

    def start_edges(out_ref, in_ref, which):
        for side, step in ((0, 1), (1, sz.ns - 1)):
            pltpu.make_async_remote_copy(
                src_ref=out_ref.at[side], dst_ref=in_ref.at[side],
                send_sem=ed_send.at[2 * which + side], recv_sem=ed_recv.at[2 * which + side],
                device_id=(g, lax.rem(s + step, sz.ns)), device_id_type=MESH,
            ).start()

    def wait_edges(ref, sems, which):
        for side in range(2):
            pltpu.make_async_copy(ref.at[side], ref.at[side], sems.at[2 * which + side]).wait()

    def start_fringe(out_ref, in_ref, which):
        in_ref[g] = out_ref[g]

        def send(p):
            pltpu.make_async_remote_copy(
                src_ref=out_ref.at[p], dst_ref=in_ref.at[g],
                send_sem=fr_send.at[which], recv_sem=fr_recv.at[which],
                device_id=(p, s), device_id_type=MESH,
            ).start()

        each_grid_peer(send)

    def wait_many(ref, number, sem):
        pltpu.make_async_copy(ref.at[pl.ds(0, number)], ref.at[pl.ds(0, number)], sem).wait()

    def own_terms(field_ref, out_ref):
        low_half = lane_ids((HALF, LANES)) < HALF
        for v in range(var_count):
            field = field_ref[v]
            flipped = swap_halves(field)
            left, right = jnp.where(low_half, field, flipped), jnp.where(low_half, flipped, field)
            for a in range(var_count):
                term = jeff_ref[1, a, v:v + 1, :] * left + jeff_ref[2, a, v:v + 1, :] * right
                out_ref[a] = term if v == 0 else out_ref[a] + term

    def edge_terms(in_ref, out_ref):
        low_half = lane_ids((PACK, LANES)) < HALF
        for v in range(var_count):
            spread = []
            for side in range(2):
                packed = in_ref[side, v]
                flipped = swap_halves(packed)
                spread.append(jnp.concatenate(
                    [jnp.where(low_half, packed, flipped), jnp.where(low_half, flipped, packed)], axis=0))
            for a in range(var_count):
                term = jeff_ref[0, a, v:v + 1, :] * spread[0] + jeff_ref[3, a, v:v + 1, :] * spread[1]
                out_ref[a] = out_ref[a] + term

    def fringe_terms(in_ref, out_ref, chunk):
        left = []
        for k in range(len(chunk)):
            turned = jnp.transpose(in_ref[:, k, :])
            left.append(jnp.concatenate([turned[:HALF], turned[HALF:]], axis=1))
        lh, ll = halves(jnp.concatenate(left, axis=0))
        scatter = scatter_ref[...]
        total = dot1(lh, scatter, NN) + dot1(ll, scatter, NN)
        for k, v in enumerate(chunk):
            out_ref[v] = out_ref[v] + total[HALF * k:HALF * (k + 1)]

    loads["x"].wait()
    for k, chunk in enumerate(CHUNKS):
        fill_fringe(x_ref, send1[k], chunk)
    send1[0][:, len(CHUNKS[0]), :] = cell_row
    fill_edges(x_ref, edge_out1)
    pl.semaphore_wait(barrier, sz.grid - 1 + sz.ns - 1)
    for k in range(count):
        start_fringe(send1[k], got1[k], k)
    start_edges(edge_out1, edge_in1, 0)

    loads["jac"].wait()
    loads["cols"].wait()
    side_on = [(s > 0).astype(F32), F32(1.0), F32(1.0), (s < sz.ns - 1).astype(F32)]
    listed = jac_ref.shape[3]
    low_lane = lane_ids((listed, LANES)) < HALF
    turn = row_ids((listed, LANES))
    picks = []
    for j in range(4):
        pick = jnp.zeros((listed, LANES), F32)
        for k in range(listed):
            left, right = [jnp.where(cols_ref[i, k] == j, side_on[j], F32(0.0)) for i in range(2)]
            pick = jnp.where(turn == k, jnp.where(low_lane, left, right), pick)
        picks.append(pick)
    for a in range(var_count):
        for b in range(var_count):
            both = jnp.concatenate([jac_ref[0, a, b], jac_ref[1, a, b]], axis=1)
            for j in range(4):
                jeff_ref[j, a, b:b + 1, :] = jnp.sum(picks[j] * both, axis=0, keepdims=True)

    own_terms(x_ref, v_ref)
    wait_edges(edge_in1, ed_recv, 0)
    edge_terms(edge_in1, v_ref)

    for k, chunk in enumerate(CHUNKS):
        wait_many(got1[k], sz.grid - 1, fr_recv.at[k])
        if k == 0:
            cells = got1[0][:, len(chunk), :]
            numbers = (lanes + 1).astype(F32)
            scatter_ref[...] = jnp.concatenate(
                [(cells[:, j * HALF:j * HALF + 1] == numbers).astype(F32) for j in range(2)], axis=0
            ).astype(BF16)
        fringe_terms(got1[k], v_ref, chunk)
        fill_fringe(v_ref, send2[k], chunk)
        start_fringe(send2[k], got2[k], count + k)
    fill_edges(v_ref, edge_out2)
    start_edges(edge_out2, edge_in2, 1)

    def reduce_start(part, a_buf, which):
        mine = me1 * sz.share
        a_buf[me1] = part[pl.ds(mine, sz.share)]

        for column, slab in first_of:
            q = lax.div(column, sz.nc) * sz.ns + slab
            pltpu.make_async_remote_copy(
                src_ref=part.at[pl.ds(q * sz.share, sz.share)], dst_ref=a_buf.at[me1],
                send_sem=red_send.at[which], recv_sem=red_recv.at[which],
                device_id=(rows_of[-1] + column + core, slab), device_id_type=MESH,
            ).start()

    def reduce_middle(a_buf, mid, b_buf, which):
        wait_many(a_buf, sz.first - 1, red_recv.at[which])
        value = a_buf[0]
        for i in range(1, sz.first):
            value = value + a_buf[i]
        mid[...] = value
        b_buf[me2] = value

        for place in second_of:
            pltpu.make_async_remote_copy(
                src_ref=mid, dst_ref=b_buf.at[me2],
                send_sem=red_send.at[which + 1], recv_sem=red_recv.at[which + 1],
                device_id=(place + columns_of[-1], s), device_id_type=MESH,
            ).start()

    def reduce_last(b_buf, sum_buf, all_buf, which):
        wait_many(b_buf, sz.second - 1, red_recv.at[which + 1])
        value = b_buf[0]
        for i in range(1, sz.second):
            value = value + b_buf[i]
        sum_buf[...] = value
        all_buf[me1] = value

        for column, slab in first_of:
            pltpu.make_async_remote_copy(
                src_ref=sum_buf, dst_ref=all_buf.at[me1],
                send_sem=red_send.at[which + 2], recv_sem=red_recv.at[which + 2],
                device_id=(rows_of[-1] + column + core, slab), device_id_type=MESH,
            ).start()

    def reduced(all_buf, which):
        wait_many(all_buf, sz.first - 1, red_recv.at[which + 2])
        scale = 1.0 / sz.total_rows
        return [all_buf[:, :, t, :].reshape(PACK, LANES) * scale for t in range(3)]

    low_half = lane_ids((PACK, LANES)) < HALF
    wide_x = wide(x_ref)
    wide_v = wide(v_ref)
    pair = jnp.concatenate([wide_x, wide_v], axis=0)
    early = dot3(pair, pair, NT)
    part_e[:, 0, :] = early[:PACK]
    part_e[:, 1, :] = early[PACK:HALF]
    part_e[:, 2, :] = jnp.where(low_half, swap_halves(early[HALF:HALF + PACK]), early[HALF + PACK:])
    reduce_start(part_e, a_e, 0)
    own_terms(v_ref, u_ref)
    wait_edges(edge_in2, ed_recv, 1)
    edge_terms(edge_in2, u_ref)
    late = jnp.zeros((3 * HALF, HALF), F32)
    for k, chunk in enumerate(CHUNKS):
        wait_many(got2[k], sz.grid - 1, fr_recv.at[count + k])
        fringe_terms(got2[k], u_ref, chunk)
        parts = [jnp.concatenate([ref[v] for v in chunk], axis=1) for ref in (x_ref, v_ref, u_ref)]
        late = late + dot3(jnp.concatenate(parts, axis=0), parts[2], NT)
    for t in range(3):
        block = late[HALF * t:HALF * (t + 1)]
        part_l[:, t, :] = jnp.concatenate([block[:PACK], block[PACK:]], axis=1)
    reduce_start(part_l, a_l, 3)
    reduce_middle(a_e, mid_e, b_e, 0)
    reduce_middle(a_l, mid_l, b_l, 3)
    reduce_last(b_e, sum_e, all_e, 0)
    reduce_last(b_l, sum_l, all_l, 3)

    top, bottom, third = reduced(all_e, 0)
    own = jnp.concatenate([top[:, :HALF], bottom[:, :HALF]], axis=0)
    with_v = jnp.concatenate([top[:, HALF:], bottom[:, HALF:]], axis=0)
    eye = (row_ids((HALF, HALF)) == lane_ids((HALF, HALF))).astype(F32)
    proj_1 = own + with_v
    lack_1 = eye - proj_1
    left_1 = with_v + dot3(own, lack_1, NN)
    gram_11 = split_rows(third) + dot3(
        jnp.concatenate([with_v, lack_1], axis=0), jnp.concatenate([lack_1, left_1], axis=0), TN)
    factor_11, inverse_11 = eliminate(gram_11)
    wide_u = wide(u_ref)
    basis_1 = dot3(inverse_11, wide_v + dot3(lack_1, wide_x, TN), NN)
    for v in range(var_count):
        basis_ref[0, v] = basis_1[:, LANES * v:LANES * (v + 1)]
    solver = jnp.concatenate(
        [inverse_11, dot3(inverse_11, left_1, NT), dot3(inverse_11, lack_1, NT)], axis=1)

    with_u, cross, square = [split_rows(value) for value in reduced(all_l, 3)]
    lack_3 = (own - eye) - with_u
    left_3 = with_u + dot3(own, lack_3, NN)
    factor_13 = dot3(solver, jnp.concatenate([cross, lack_3, with_u], axis=0), NN)
    gram_33 = square + dot3(
        jnp.concatenate([with_u, lack_3], axis=0), jnp.concatenate([lack_3, left_3], axis=0), TN)
    factor_22, inverse_22 = eliminate(gram_33 - dot3(factor_13, factor_13, TN))
    rest = wide_u + dot3(
        jnp.concatenate([lack_3, -factor_13], axis=0), jnp.concatenate([wide_x, basis_1], axis=0), TN)
    basis_2 = dot3(inverse_22, rest, NN)
    for v in range(var_count):
        basis_ref[1, v] = basis_2[:, LANES * v:LANES * (v + 1)]
    proj_ref[...] = jnp.concatenate([proj_1, (proj_1 + with_v) + with_u], axis=1)
    factor_ref[...] = jnp.concatenate([
        jnp.concatenate([factor_11, 2.0 * factor_11 + factor_13], axis=1),
        jnp.concatenate([jnp.zeros((HALF, HALF), F32), factor_22], axis=1),
    ], axis=0)

    wait_edges(edge_out1, ed_send, 0)
    wait_edges(edge_out2, ed_send, 1)
    for k in range(count):
        wait_many(send1[k], sz.grid - 1, fr_send.at[k])
        wait_many(send2[k], sz.grid - 1, fr_send.at[count + k])
    for which, (a_buf, b_buf, all_buf) in ((0, (a_e, b_e, all_e)), (3, (a_l, b_l, all_l))):
        wait_many(a_buf, sz.first - 1, red_send.at[which])
        wait_many(b_buf, sz.second - 1, red_send.at[which + 1])
        wait_many(all_buf, sz.first - 1, red_send.at[which + 2])


def write_out(basis_ref, proj_ref, factor_ref, basis_hbm, proj_hbm, factor_hbm, sems):
    pairs = ((basis_ref, basis_hbm), (proj_ref, proj_hbm), (factor_ref, factor_hbm))
    copies = [pltpu.make_async_copy(source, target, sems.at[k]) for k, (source, target) in enumerate(pairs)]
    for copy in copies:
        copy.start()
    for copy in copies:
        copy.wait()


def shards(sz, start_block, jacobian, block_cols, donor_cell, donor_weight, fringe_dest, recv_cell):
    var_count, rhs_count, cell_count = start_block.shape
    vmem = pl.BlockSpec(memory_space=pltpu.VMEM)
    field = (var_count, rhs_count, cell_count)
    edge = pltpu.VMEM((2, var_count, PACK, LANES), F32)
    sums = [
        pltpu.VMEM((PACK, 3, LANES), F32),
        pltpu.VMEM((sz.first, sz.share, 3, LANES), F32),
        pltpu.VMEM((sz.share, 3, LANES), F32),
        pltpu.VMEM((sz.second, sz.share, 3, LANES), F32),
        pltpu.VMEM((sz.share, 3, LANES), F32),
        pltpu.VMEM((sz.first, sz.share, 3, LANES), F32),
    ]
    inputs = (
        block_cols,
        start_block,
        jnp.transpose(jacobian, (0, 2, 3, 1, 4)),
        donor_cell.T,
        donor_weight.T,
        fringe_dest.reshape(1, -1),
        recv_cell.reshape(1, -1),
    )
    places = [pltpu.SMEM] + [pltpu.VMEM] * 6
    count = len(CHUNKS)
    first_chunks = [pltpu.VMEM((LANES, len(c) + (k == 0), LANES), F32) for k, c in enumerate(CHUNKS)]
    second_chunks = [pltpu.VMEM((LANES, len(c), LANES), F32) for c in CHUNKS]
    results = pl.pallas_call(
        functools.partial(kernel, sz),
        out_shape=(
            jax.ShapeDtypeStruct((2,) + field, F32),
            jax.ShapeDtypeStruct((rhs_count, 2 * rhs_count), F32),
            jax.ShapeDtypeStruct((2 * rhs_count, 2 * rhs_count), F32),
        ),
        in_specs=[pl.BlockSpec(memory_space=HBM)] * 7,
        out_specs=(vmem, vmem, vmem),
        scratch_shapes=[
            *[place(value.shape, value.dtype) for place, value in zip(places, inputs)],
            pltpu.SemaphoreType.DMA((7,)),
            pltpu.VMEM(field, F32),
            pltpu.VMEM(field, F32),
            pltpu.VMEM((4, var_count, 8, LANES), F32),
            pltpu.VMEM((LANES, 2 * LANES), BF16),
            pltpu.VMEM((LANES, 2 * LANES), BF16),
            pltpu.VMEM((2 * LANES, LANES), BF16),
            edge, edge, edge, edge,
            *sums, *sums,
            pltpu.SemaphoreType.DMA((2 * count,)),
            pltpu.SemaphoreType.DMA((2 * count,)),
            pltpu.SemaphoreType.DMA((4,)),
            pltpu.SemaphoreType.DMA((4,)),
            pltpu.SemaphoreType.DMA((6,)),
            pltpu.SemaphoreType.DMA((6,)),
            *first_chunks, *first_chunks, *second_chunks, *second_chunks,
        ],
        compiler_params=pltpu.CompilerParams(
            collective_id=0, has_side_effects=True, vmem_limit_bytes=32 * 1024 * 1024
        ),
    )(*[pltpu.with_memory_space_constraint(value, HBM) for value in inputs])
    return pl.pallas_call(
        write_out,
        out_shape=tuple(jax.ShapeDtypeStruct(value.shape, value.dtype) for value in results),
        in_specs=[vmem] * 3,
        out_specs=(pl.BlockSpec(memory_space=HBM),) * 3,
        scratch_shapes=[pltpu.SemaphoreType.DMA((3,))],
        compiler_params=pltpu.CompilerParams(vmem_limit_bytes=2 * 1024 * 1024),
    )(*results)


def solution(mesh):
    grid, slab = mesh.shape["grid"], mesh.shape["slab"]
    side = 8 if grid == 128 else 1
    sz = Sizes(grid // (2 * side), side, 2, slab, 5 * 128 * grid * slab)
    both = ("grid", "slab")
    in_specs = (
        P(None, None, both),
        P(both, None, None, None, None),
        P(both, None),
        P(both, None),
        P(both, None),
        P(both, None),
        P(both),
    )
    out_specs = (P(None, None, None, both), P(), P())
    return jax.shard_map(
        functools.partial(shards, sz), mesh=mesh, in_specs=in_specs, out_specs=out_specs, check_vma=False
    )
```
